256 devices in a mesh: shard: 128 (over y, x, z), rep: 2 (over core).
Axes of the slice: x: 4, y: 4, z: 8, core: 2. Of those that a mesh axis runs over, the one named last changes fastest.
Arguments:
- embeddings: bfloat16 [131072, 1024], P('shard')
- labels: int32 [131072], P('shard'), may hold values from 0 to 2047, as said below
Outputs:
- density: float32 [131072], P('shard')
The draws below stay inside these ranges and needn't reach their ends.
Inputs may be any that keep to these rules, and one draw needn't show every extreme that they name: `labels`: in each aligned block of 1024 documents (those of one index of shard) at most 1 name any one cluster, and in every block some cluster is named by exactly 1; so a cluster holds at most 128 documents, and some cluster holds exactly 128.
All inputs are finite; a program needn't handle non-finite values.
Results may differ from the reference program's by a relative error of at most 0.00038.
Values may be sent and summed in bfloat16 or wider, within the bound.
A program may use at most 64 MiB of HBM per device.

```python
import math
import jax
import jax.numpy as jnp
from jax import lax

D = 1024
CAP = 128
DOC_DEV = 1024
MAX_CLUSTER_DOCS = 1
DOCS = 131072
KMEANS_GROUPS = 2048
N_SHARD = 128


def label_table(key):
    key = jax.random.fold_in(key, 11)
    random_keys = jax.random.split(key, 4)
    position_total = KMEANS_GROUPS * MAX_CLUSTER_DOCS
    cluster_reward = jax.random.randint(random_keys[0], (KMEANS_GROUPS,), 0, 2 ** 13)
    giants = jax.random.randint(random_keys[1], (2,), 0, KMEANS_GROUPS)
    cluster_ids = jnp.arange(KMEANS_GROUPS, dtype=jnp.int32)
    oversized_flag = (cluster_ids == giants[0]) | (cluster_ids == giants[1])
    cluster_reward = jnp.where(oversized_flag, 2 ** 15, cluster_reward)
    position_index = jnp.arange(position_total, dtype=jnp.int32)
    random_share = jax.random.randint(random_keys[2], (N_SHARD, position_total), 0, 2 ** 14)
    position_priority = (random_share + cluster_reward[position_index // MAX_CLUSTER_DOCS][None, :]) * position_total + position_index[None, :]
    chosen = lax.top_k(position_priority, DOC_DEV)[1]
    shuffle = jax.random.permutation(random_keys[3], DOC_DEV)
    chosen = chosen[:, shuffle]
    return (chosen // MAX_CLUSTER_DOCS).reshape(-1).astype(jnp.int32)


def draw_labels(key, part):
    return label_table(key)


def draw_embeddings(key, part):
    labels = label_table(key)
    key = jax.random.fold_in(key, 5)
    random_keys = jax.random.split(key, 10)
    centers = jax.random.normal(random_keys[0], (KMEANS_GROUPS, D), jnp.float32)
    mixing = jnp.exp(jax.random.uniform(random_keys[1], (DOCS, 1), jnp.float32, math.log(0.5), math.log(1.0)))
    coarse = jax.random.randint(random_keys[6], (DOCS,), 0, 64)
    shift_count = jax.random.randint(random_keys[7], (DOCS,), 0, 8)
    subgroup = jnp.right_shift(coarse, shift_count)
    group_id = labels * 64 + subgroup
    base_key = random_keys[8]
    bases = jax.vmap(lambda group: jax.random.normal(jax.random.fold_in(base_key, group), (D,), jnp.float32))(group_id)
    closeness = 1.25 * jnp.exp(jax.random.uniform(random_keys[9], (DOCS, 1), jnp.float32, math.log(0.05), math.log(0.25)))
    scatter_part = jax.random.normal(random_keys[2], (DOCS, D), jnp.float32)
    row_scale = jnp.exp(jax.random.uniform(random_keys[3], (DOCS, 1), jnp.float32, 0.0, math.log(10.0)))
    col_scale = jnp.exp(jax.random.uniform(random_keys[4], (1, D), jnp.float32, 0.0, math.log(10.0)))
    values = (mixing * centers[labels] + bases + closeness * scatter_part) * col_scale * row_scale
    return values.astype(jnp.bfloat16)


def setup_inputs(seed: int = 0) -> dict:
    key_of = jax.random.split(jax.random.key(seed), 3)
    return {
        "embeddings": draw_embeddings(jax.random.fold_in(key_of[2], 71), 0),
        "labels": draw_labels(jax.random.fold_in(key_of[2], 71), 0),
    }


sharpness = 4.0
epsilon = 1e-06

def unit_rows(embeddings):
    values = embeddings.astype(jnp.float32)
    scale = lax.rsqrt(lax.optimization_barrier(jnp.sum(values * values, axis=-1, keepdims=True)) + epsilon)
    return (values * scale).astype(jnp.bfloat16)

def slot_ranks(labels):
    doc_order = jnp.argsort(labels, stable=True).astype(jnp.int32)
    sorted_labels = labels[doc_order]
    first_seen = jnp.searchsorted(sorted_labels, sorted_labels, side='left').astype(jnp.int32)
    sorted_rank = jnp.arange(labels.shape[0], dtype=jnp.int32) - first_seen
    return jnp.zeros_like(labels).at[doc_order].set(sorted_rank)

def reference(embeddings, labels):
    unit = unit_rows(embeddings)
    ranks = slot_ranks(labels)
    table = jnp.full((KMEANS_GROUPS, CAP), DOCS, jnp.int32).at[labels, ranks].set(jnp.arange(DOCS, dtype=jnp.int32))
    padded = jnp.concatenate([unit, jnp.zeros((1, D), jnp.bfloat16)], axis=0)
    off_diagonal = 1.0 - jnp.eye(CAP, dtype=jnp.float32)

    def per_cluster(members):
        member_rows = padded[members].astype(jnp.float32)
        gram = jnp.dot(member_rows, member_rows.T, precision=lax.Precision.HIGHEST)
        present = (members < DOCS).astype(jnp.float32)
        weights = jnp.exp(sharpness * (gram - 1.0)) * present[None, :] * off_diagonal
        return lax.optimization_barrier(jnp.sum(weights, axis=1))
    totals = lax.map(per_cluster, table)
    return jnp.log1p(totals[labels, ranks])
```

```python
import functools
import jax
import jax.numpy as jnp
from jax import lax
from jax.experimental import pallas as pl
from jax.experimental.pallas import tpu as pltpu
from jax.sharding import PartitionSpec as P

SHARDS = 128
DOCS_DEV = 1024
D = 1024
CL = 8
GROUPS = 4
GROUP_Q = SHARDS // GROUPS
ROWS = GROUP_Q * CL

sharpness = 4.0
epsilon = 1e-06


def offset_of(q):
    k = q % 8
    dz = jnp.where(k % 2 == 1, (k + 1) // 2, (8 - k // 2) % 8)
    return (q // 32) % 4, (q // 8) % 4, dz


def q_of(dy, dx, dz):
    k = jnp.where(dz == 0, 0, jnp.where(dz <= 4, 2 * dz - 1, 2 * (8 - dz)))
    return dy * 32 + dx * 8 + k


def shift(s, q, sign):
    dy, dx, dz = offset_of(q)
    y = (s // 32 + 4 + sign * dy) % 4
    x = (s // 8 % 4 + 4 + sign * dx) % 4
    z = (s % 8 + 8 + sign * dz) % 8
    return y * 32 + x * 8 + z


def kernel(e_hbm, labels_ref, out_ref, e_ref, send, recv, unit, tot, ret, halves,
           load_sem, send_sem, recv_sem, back_send, back_recv, half_sem):
    me = lax.axis_index("shard")
    rep = lax.axis_index("rep")
    load = pltpu.make_async_copy(e_hbm, e_ref, load_sem)
    load.start()

    barrier = pltpu.get_barrier_semaphore()

    def greet(q, _):
        pl.semaphore_signal(barrier, inc=1, device_id={"shard": shift(me, q, -1)})
        return 0

    lax.fori_loop(1, SHARDS, greet, 0)
    pl.semaphore_signal(barrier, inc=1, device_id={"rep": 1 - rep})
    load.wait()

    labels = labels_ref[...]
    owner = labels // 16
    dy = (owner // 32 - me // 32 + 4) % 4
    dx = (owner // 8 % 4 - me // 8 % 4 + 4) % 4
    dz = (owner % 8 - me % 8 + 8) % 8
    doc_q = q_of(dy, dx, dz)
    doc_slot = jnp.where(labels % 16 // 8 == rep, doc_q * 8 + labels % 8, -1)

    def row_copy(q):
        return pltpu.make_async_remote_copy(
            src_ref=send.at[q], dst_ref=recv.at[q], send_sem=send_sem,
            recv_sem=recv_sem.at[q // GROUP_Q],
            device_id={"shard": shift(me, q, 1)})

    def back_copy(q):
        return pltpu.make_async_remote_copy(
            src_ref=tot.at[q // 16], dst_ref=ret.at[q], send_sem=back_send,
            recv_sem=back_recv, device_id={"shard": shift(me, q, -1)})

    def fill(g):
        ids = lax.broadcasted_iota(jnp.int32, (ROWS, 128), 0) + g * ROWS
        hits = [ids == doc_slot[j:j + 1, :] for j in range(8)]
        onehot = jnp.concatenate(
            [jnp.where(h, 1.0, 0.0).astype(jnp.bfloat16) for h in hits], axis=1)
        any_hit = functools.reduce(
            jnp.add, [jnp.where(h, 1.0, 0.0) for h in hits])
        present = jnp.sum(any_hit, axis=1, keepdims=True) > 0.0
        rows = jnp.dot(onehot, e_ref[...], preferred_element_type=jnp.float32)
        rows = jnp.where(present, rows, jnp.nan)
        rows = rows.reshape(GROUP_Q, CL, D).astype(jnp.bfloat16)
        send[g * GROUP_Q:(g + 1) * GROUP_Q] = rows
        if g == 0:
            recv[0] = rows[0]

    for g in range(GROUPS):
        fill(g)
        if g == 0:
            pl.semaphore_wait(barrier, SHARDS)

        def push(q, _):
            row_copy(q).start()
            return 0

        lax.fori_loop(1 if g == 0 else g * GROUP_Q, (g + 1) * GROUP_Q, push, 0)

    row_id = lax.broadcasted_iota(jnp.int32, (ROWS, ROWS), 0)
    col_id = lax.broadcasted_iota(jnp.int32, (ROWS, ROWS), 1)
    same = row_id % CL == col_id % CL
    same_off = same & (row_id != col_id)

    def weights(a, b, mask):
        gram = lax.dot_general(a, b, (((1,), (1,)), ((), ())),
                               preferred_element_type=jnp.float32)
        ok = mask & (gram == gram)
        w = jnp.where(ok, jnp.exp(sharpness * (gram - 1.0)), 0.0)
        return jnp.sum(w, axis=0, keepdims=True)

    totals = [jnp.zeros((1, ROWS), jnp.float32) for _ in range(GROUPS)]
    for g in range(GROUPS):
        lo = 1 if g == 0 else g * GROUP_Q
        block = pl.ds(lo, (g + 1) * GROUP_Q - lo)
        pltpu.make_async_copy(recv.at[block], recv.at[block], recv_sem.at[g]).wait()
        values = recv[g * GROUP_Q:(g + 1) * GROUP_Q].astype(jnp.float32).reshape(ROWS, D)
        scale = lax.rsqrt(jnp.sum(values * values, axis=1, keepdims=True) + epsilon)
        mine = (values * scale).astype(jnp.bfloat16)
        unit[g * ROWS:(g + 1) * ROWS] = mine
        totals[g] += weights(mine, mine, same_off)
        for h in range(g):
            other = unit[h * ROWS:(h + 1) * ROWS]
            totals[g] += weights(other, mine, same)
            totals[h] += weights(mine, other, same)

    for j in range(8):
        g, part = j // 2, j % 2
        tot[j] = totals[g][:, part * 128:(part + 1) * 128]
    ret[0] = tot[0]

    def push_back(q, _):
        back_copy(q).start()
        return 0

    lax.fori_loop(1, SHARDS, push_back, 0)
    everything = pl.ds(1, SHARDS - 1)
    pltpu.make_async_copy(ret.at[everything], ret.at[everything], back_recv).wait()

    got = ret[...].reshape(SHARDS, 128)
    q_id = lax.broadcasted_iota(jnp.int32, (SHARDS, 128), 0)
    lane = lax.broadcasted_iota(jnp.int32, (SHARDS, 128), 1)
    got = jnp.where(lane // CL == q_id % 16, got, 0.0).T
    halves[rep] = jnp.sum(got.reshape(16, CL, 128), axis=0)
    swap = pltpu.make_async_remote_copy(
        src_ref=halves.at[rep], dst_ref=halves.at[rep], send_sem=half_sem.at[0],
        recv_sem=half_sem.at[1], device_id={"rep": 1 - rep})
    swap.start()
    swap.wait()

    value = jnp.zeros((8, 128), jnp.float32)
    cluster = labels % 16
    for c in range(16):
        line = jnp.broadcast_to(halves[c // 8, c % 8:c % 8 + 1, :], (8, 128))
        value = jnp.where(cluster == c, jnp.take_along_axis(line, doc_q, axis=1), value)
    out_ref[...] = value

    pltpu.make_async_copy(send.at[everything], send.at[everything], send_sem).wait()
    pltpu.make_async_copy(ret.at[everything], ret.at[everything], back_send).wait()


def local(embeddings, labels):
    totals = pl.pallas_call(
        kernel,
        out_shape=jax.ShapeDtypeStruct((8, 128), jnp.float32),
        in_specs=[pl.BlockSpec(memory_space=pl.ANY), pl.BlockSpec(memory_space=pltpu.VMEM)],
        out_specs=pl.BlockSpec(memory_space=pltpu.VMEM),
        scratch_shapes=[
            pltpu.VMEM((DOCS_DEV, D), jnp.bfloat16),
            pltpu.VMEM((SHARDS, CL, D), jnp.bfloat16),
            pltpu.VMEM((SHARDS, CL, D), jnp.bfloat16),
            pltpu.VMEM((SHARDS * CL, D), jnp.bfloat16),
            pltpu.VMEM((8, 1, 128), jnp.float32),
            pltpu.VMEM((SHARDS, 1, 128), jnp.float32),
            pltpu.VMEM((2, 8, 128), jnp.float32),
            pltpu.SemaphoreType.DMA,
            pltpu.SemaphoreType.DMA,
            pltpu.SemaphoreType.DMA((GROUPS,)),
            pltpu.SemaphoreType.DMA,
            pltpu.SemaphoreType.DMA,
            pltpu.SemaphoreType.DMA((2,)),
        ],
        compiler_params=pltpu.CompilerParams(
            collective_id=0, has_side_effects=True, vmem_limit_bytes=48 * 1024 * 1024),
        name="cluster_totals",
    )(embeddings, labels.reshape(8, 128))
    return jnp.log1p(totals.reshape(DOCS_DEV))


def solution(mesh):
    return jax.shard_map(
        local,
        mesh=mesh,
        in_specs=(P("shard", None), P("shard")),
        out_specs=P("shard"),
        check_vma=False,
    )
```

```python
import functools
import jax
import jax.numpy as jnp
from jax import lax
from jax.experimental import pallas as pl
from jax.experimental.pallas import tpu as pltpu
from jax.sharding import PartitionSpec as P

SHARDS = 128
DOCS_DEV = 1024
D = 1024
CL = 8
GROUPS = 4
GROUP_Q = SHARDS // GROUPS
ROWS = GROUP_Q * CL

sharpness = 4.0
epsilon = 1e-06


def offset_of(q):
    k = q % 8
    dz = jnp.where(k % 2 == 1, (k + 1) // 2, (8 - k // 2) % 8)
    return (q // 32) % 4, (q // 8) % 4, dz


def q_of(dy, dx, dz):
    k = jnp.where(dz == 0, 0, jnp.where(dz <= 4, 2 * dz - 1, 2 * (8 - dz)))
    return dy * 32 + dx * 8 + k


def shift(s, q, sign):
    dy, dx, dz = offset_of(q)
    y = (s // 32 + 4 + sign * dy) % 4
    x = (s // 8 % 4 + 4 + sign * dx) % 4
    z = (s % 8 + 8 + sign * dz) % 8
    return y * 32 + x * 8 + z


def kernel(e_hbm, labels_ref, out_ref, e_ref, send, recv, unit, tot, ret, halves,
           load_sem, send_sem, recv_sem, back_send, back_recv, half_sem):
    me = lax.axis_index("shard")
    rep = lax.axis_index("rep")
    load = pltpu.make_async_copy(e_hbm, e_ref, load_sem)
    load.start()

    barrier = pltpu.get_barrier_semaphore()

    def greet(q, _):
        pl.semaphore_signal(barrier, inc=1, device_id={"shard": shift(me, q, -1)})
        return 0

    lax.fori_loop(1, SHARDS, greet, 0)
    pl.semaphore_signal(barrier, inc=1, device_id={"rep": 1 - rep})
    load.wait()

    labels = labels_ref[...]
    owner = labels // 16
    dy = (owner // 32 - me // 32 + 4) % 4
    dx = (owner // 8 % 4 - me // 8 % 4 + 4) % 4
    dz = (owner % 8 - me % 8 + 8) % 8
    doc_q = q_of(dy, dx, dz)
    doc_slot = jnp.where(labels % 16 // 8 == rep, doc_q * 8 + labels % 8, -1)

    def row_copy(q):
        return pltpu.make_async_remote_copy(
            src_ref=send.at[q], dst_ref=recv.at[q], send_sem=send_sem,
            recv_sem=recv_sem.at[q // GROUP_Q],
            device_id={"shard": shift(me, q, 1)})

    def back_copy(q):
        return pltpu.make_async_remote_copy(
            src_ref=tot.at[q // 16], dst_ref=ret.at[q], send_sem=back_send,
            recv_sem=back_recv, device_id={"shard": shift(me, q, -1)})

    def fill(g):
        ids = lax.broadcasted_iota(jnp.int32, (ROWS, 128), 0) + g * ROWS
        hits = [ids == doc_slot[j:j + 1, :] for j in range(8)]
        onehot = jnp.concatenate(
            [jnp.where(h, 1.0, 0.0).astype(jnp.bfloat16) for h in hits], axis=1)
        any_hit = functools.reduce(
            jnp.add, [jnp.where(h, 1.0, 0.0) for h in hits])
        present = jnp.sum(any_hit, axis=1, keepdims=True) > 0.0
        rows = jnp.dot(onehot, e_ref[...], preferred_element_type=jnp.float32)
        rows = jnp.where(present, rows, jnp.nan)
        rows = rows.reshape(GROUP_Q, CL, D).astype(jnp.bfloat16)
        send[g * GROUP_Q:(g + 1) * GROUP_Q] = rows
        if g == 0:
            recv[0] = rows[0]

    for g in range(GROUPS):
        fill(g)
        if g == 0:
            pl.semaphore_wait(barrier, SHARDS)

        def push(q, _):
            row_copy(q).start()
            return 0

        lax.fori_loop(1 if g == 0 else g * GROUP_Q, (g + 1) * GROUP_Q, push, 0)

    row_id = lax.broadcasted_iota(jnp.int32, (ROWS, ROWS), 0)
    col_id = lax.broadcasted_iota(jnp.int32, (ROWS, ROWS), 1)
    same = row_id % CL == col_id % CL
    same_off = same & (row_id != col_id)

    def weights(a, b, mask):
        gram = lax.dot_general(a, b, (((1,), (1,)), ((), ())),
                               preferred_element_type=jnp.float32)
        ok = mask & (gram == gram)
        w = jnp.where(ok, jnp.exp(sharpness * (gram - 1.0)), 0.0)
        return jnp.sum(w, axis=0, keepdims=True)

    totals = [jnp.zeros((1, ROWS), jnp.float32) for _ in range(GROUPS)]
    for g in range(GROUPS):
        lo = 1 if g == 0 else g * GROUP_Q
        block = pl.ds(lo, (g + 1) * GROUP_Q - lo)
        pltpu.make_async_copy(recv.at[block], recv.at[block], recv_sem.at[g]).wait()
        values = recv[g * GROUP_Q:(g + 1) * GROUP_Q].astype(jnp.float32).reshape(ROWS, D)
        scale = lax.rsqrt(jnp.sum(values * values, axis=1, keepdims=True) + epsilon)
        mine = (values * scale).astype(jnp.bfloat16)
        unit[g * ROWS:(g + 1) * ROWS] = mine
        totals[g] += weights(mine, mine, same_off)
        for h in range(g):
            other = unit[h * ROWS:(h + 1) * ROWS]
            totals[g] += weights(other, mine, same)
            totals[h] += weights(mine, other, same)

    for j in range(8):
        g, part = j // 2, j % 2
        tot[j] = totals[g][:, part * 128:(part + 1) * 128]
    ret[0] = tot[0]

    def push_back(q, _):
        back_copy(q).start()
        return 0

    lax.fori_loop(1, SHARDS, push_back, 0)
    everything = pl.ds(1, SHARDS - 1)
    pltpu.make_async_copy(ret.at[everything], ret.at[everything], back_recv).wait()

    got = ret[...].reshape(SHARDS, 128)
    q_id = lax.broadcasted_iota(jnp.int32, (SHARDS, 128), 0)
    lane = lax.broadcasted_iota(jnp.int32, (SHARDS, 128), 1)
    got = jnp.where(lane // CL == q_id % 16, got, 0.0).T
    halves[rep] = jnp.sum(got.reshape(16, CL, 128), axis=0)
    swap = pltpu.make_async_remote_copy(
        src_ref=halves.at[rep], dst_ref=halves.at[rep], send_sem=half_sem.at[0],
        recv_sem=half_sem.at[1], device_id={"rep": 1 - rep})
    swap.start()
    swap.wait()

    value = jnp.zeros((8, 128), jnp.float32)
    cluster = labels % 16
    for c in range(16):
        line = jnp.broadcast_to(halves[c // 8, c % 8:c % 8 + 1, :], (8, 128))
        value = jnp.where(cluster == c, jnp.take_along_axis(line, doc_q, axis=1), value)
    out_ref[...] = value

    pltpu.make_async_copy(send.at[everything], send.at[everything], send_sem).wait()
    pltpu.make_async_copy(ret.at[everything], ret.at[everything], back_send).wait()


def direct_totals(embeddings, labels):
    return pl.pallas_call(
        kernel,
        out_shape=jax.ShapeDtypeStruct((8, 128), jnp.float32),
        in_specs=[pl.BlockSpec(memory_space=pl.ANY), pl.BlockSpec(memory_space=pltpu.VMEM)],
        out_specs=pl.BlockSpec(memory_space=pltpu.VMEM),
        scratch_shapes=[
            pltpu.VMEM((DOCS_DEV, D), jnp.bfloat16),
            pltpu.VMEM((SHARDS, CL, D), jnp.bfloat16),
            pltpu.VMEM((SHARDS, CL, D), jnp.bfloat16),
            pltpu.VMEM((SHARDS * CL, D), jnp.bfloat16),
            pltpu.VMEM((8, 1, 128), jnp.float32),
            pltpu.VMEM((SHARDS, 1, 128), jnp.float32),
            pltpu.VMEM((2, 8, 128), jnp.float32),
            pltpu.SemaphoreType.DMA,
            pltpu.SemaphoreType.DMA,
            pltpu.SemaphoreType.DMA((GROUPS,)),
            pltpu.SemaphoreType.DMA,
            pltpu.SemaphoreType.DMA,
            pltpu.SemaphoreType.DMA((2,)),
        ],
        compiler_params=pltpu.CompilerParams(
            collective_id=0, has_side_effects=True, vmem_limit_bytes=48 * 1024 * 1024),
        name="cluster_totals",
    )(embeddings, labels.reshape(8, 128))


PLANE = 16
DEPTH = 8
SLOTS = PLANE * CL
PACK = 96
LAST = PACK - 1
ORDER = (1, 7, 2, 6, 3, 5, 4)


def prefix_rank(marks):
    i = lax.broadcasted_iota(jnp.int32, (SLOTS, SLOTS), 0)
    j = lax.broadcasted_iota(jnp.int32, (SLOTS, SLOTS), 1)
    before = jnp.where(i < j, 1.0, 0.0).astype(jnp.bfloat16)
    return jnp.dot(marks.astype(jnp.bfloat16), before, preferred_element_type=jnp.float32)


def pack_matrix(mark, rank):
    row = lax.broadcasted_iota(jnp.int32, (PACK, SLOTS), 0)
    hit = (row == rank.astype(jnp.int32)) & (mark > 0.0) & (row < LAST)
    return jnp.where(hit, 1.0, 0.0).astype(jnp.bfloat16)


def mark_absent(rows, mark):
    column = jnp.broadcast_to(mark, (SLOTS, SLOTS)).T
    first = jnp.where(column > 0.0, rows[:, :SLOTS], jnp.nan)
    return jnp.concatenate([first, rows[:, SLOTS:]], axis=1)


def packed_kernel(e_hbm, labels_hbm, out_ref, e_ref, labels_ref, zs, zr, ps, pr, unit, tot, r1, s2, r2,
                  load_sem, zss, zrs, pss, prs, r1s, r1r, r1c, r2s, r2r):
    me = lax.axis_index("shard")
    rep = lax.axis_index("rep")
    y, x, z = me // 32, me // 8 % 4, me % 8
    z_dev = [y * 32 + x * 8 + (z + d) % 8 for d in range(DEPTH)]
    p_dev = [(y + p // 4) % 4 * 32 + (x + p % 4) % 4 * 8 + z for p in range(PLANE)]

    load = pltpu.make_async_copy(e_hbm, e_ref, load_sem.at[0])
    load.start()
    load_labels = pltpu.make_async_copy(labels_hbm, labels_ref, load_sem.at[1])
    load_labels.start()

    barrier = pltpu.get_barrier_semaphore()
    for d in range(1, DEPTH):
        pl.semaphore_signal(barrier, inc=1, device_id={"shard": z_dev[d]})
    for p in range(1, PLANE):
        for r in range(2):
            pl.semaphore_signal(barrier, inc=1, device_id={"shard": p_dev[p], "rep": r})
    pl.semaphore_signal(barrier, inc=1, device_id={"rep": 1 - rep})
    load_labels.wait()

    labels = labels_ref[...]
    owner = labels // 16
    doc_p = (owner // 32 - y + 4) % 4 * 4 + (owner // 8 % 4 - x + 4) % 4
    doc_z = (owner % 8 - z + 8) % 8
    doc_rep = labels % 16 // 8
    doc_slot = doc_p * CL + labels % 8
    key = jnp.where(doc_rep == rep, doc_z * SLOTS + doc_slot, -1)

    ids = lax.broadcasted_iota(jnp.int32, (SLOTS, 128), 0)

    def place(d):
        return jnp.concatenate(
            [jnp.where(ids + d * SLOTS == key[j:j + 1, :], 1.0, 0.0).astype(jnp.bfloat16)
             for j in range(8)], axis=1)

    placed = [place(d) for d in range(DEPTH)]
    ones = jnp.ones((16, DOCS_DEV), jnp.bfloat16)
    marks = jnp.concatenate(
        [lax.dot_general(ones, a, (((1,), (1,)), ((), ())),
                         preferred_element_type=jnp.float32)[:1] for a in placed], axis=0)
    ranks = prefix_rank(marks)
    row_id = lax.broadcasted_iota(jnp.int32, (PACK, SLOTS), 0)

    load.wait()
    own = jnp.dot(placed[0], e_ref[...], preferred_element_type=jnp.float32)
    own = mark_absent(own, marks[:1]).reshape(PLANE, CL, D).astype(jnp.bfloat16)
    ps[0] = own
    pr[0, 0] = own[0]
    for group in ((1, 7), (2, 6), (3, 5), (4,)):
        select = jnp.concatenate(
            [jnp.dot(pack_matrix(marks[d:d + 1], ranks[d:d + 1]), placed[d],
                     preferred_element_type=jnp.float32) for d in group], axis=0)
        rows = jnp.dot(select.astype(jnp.bfloat16), e_ref[...], preferred_element_type=jnp.float32)
        for i, d in enumerate(group):
            part = rows[i * PACK:(i + 1) * PACK]
            first = jnp.where(row_id == LAST, marks[d:d + 1], part[:, :SLOTS])
            zs[d] = jnp.concatenate([first, part[:, SLOTS:]], axis=1).astype(jnp.bfloat16)

    pl.semaphore_wait(barrier, DEPTH - 1 + 2 * PLANE - 1)

    def z_copy(d):
        return pltpu.make_async_remote_copy(
            src_ref=zs.at[d], dst_ref=zr.at[d], send_sem=zss.at[d], recv_sem=zrs.at[d],
            device_id={"shard": z_dev[d]})

    def forward(d):
        for p in range(1, PLANE):
            pltpu.make_async_remote_copy(
                src_ref=ps.at[d, p], dst_ref=pr.at[d, p], send_sem=pss.at[d], recv_sem=prs.at[d],
                device_id={"shard": p_dev[p]}).start()

    others = pl.ds(1, PLANE - 1)
    for d in ORDER:
        z_copy(d).start()
    forward(0)

    full = [jnp.zeros((1, SLOTS), jnp.float32)]

    def expand(d):
        pltpu.make_async_copy(zr.at[d], zr.at[d], zrs.at[d]).wait()
        mark = zr[d, PACK - 16:PACK, :SLOTS].astype(jnp.float32)[15:16]
        rank = prefix_rank(jnp.broadcast_to(mark, (16, SLOTS)))[:1]
        full[0] = jnp.maximum(full[0], rank + mark)
        rows = lax.dot_general(pack_matrix(mark, rank), zr[d], (((0,), (0,)), ((), ())),
                               preferred_element_type=jnp.float32)
        rows = mark_absent(rows, mark).reshape(PLANE, CL, D).astype(jnp.bfloat16)
        ps[d] = rows
        pr[d, 0] = rows[0]
        forward(d)

    i = lax.broadcasted_iota(jnp.int32, (SLOTS, SLOTS), 0)
    j = lax.broadcasted_iota(jnp.int32, (SLOTS, SLOTS), 1)
    same = i % CL == j % CL
    same_off = same & (i != j)

    def weights(a, b, mask):
        gram = lax.dot_general(a, b, (((1,), (1,)), ((), ())),
                               preferred_element_type=jnp.float32)
        ok = mask & (gram == gram)
        w = jnp.where(ok, jnp.exp(sharpness * (gram - 1.0)), 0.0)
        return jnp.sum(w, axis=0, keepdims=True)

    totals = {}
    done = []

    def process(d):
        k = len(done)
        pltpu.make_async_copy(pr.at[d, others], pr.at[d, others], prs.at[d]).wait()
        values = pr[d].astype(jnp.float32).reshape(SLOTS, D)
        scale = lax.rsqrt(jnp.sum(values * values, axis=1, keepdims=True) + epsilon)
        mine = (values * scale).astype(jnp.bfloat16)
        unit[k * SLOTS:(k + 1) * SLOTS] = mine
        total = weights(mine, mine, same_off)
        if k:
            before = unit[:k * SLOTS]
            total += weights(before, mine, jnp.concatenate([same] * k, axis=0))
            rest = weights(mine, before, jnp.concatenate([same] * k, axis=1))
            for n, e in enumerate(done):
                totals[e] += rest[:, n * SLOTS:(n + 1) * SLOTS]
        totals[d] = total
        done.append(d)

    expand(1)
    expand(7)
    process(0)
    expand(2)
    expand(6)
    process(1)
    process(7)
    expand(3)
    expand(5)
    process(2)
    process(6)
    expand(4)
    process(3)
    process(5)
    process(4)

    table = jnp.concatenate([totals[d] for d in range(DEPTH)], axis=0)
    table = jnp.where(jnp.max(full[0], axis=1, keepdims=True) > float(LAST), -1.0, table)
    tot[...] = table

    def back_one(p, r):
        return pltpu.make_async_remote_copy(
            src_ref=tot, dst_ref=r1.at[(4 - p // 4) % 4 * 4 + (4 - p % 4) % 4, rep], send_sem=r1s, recv_sem=r1r,
            device_id={"shard": p_dev[p], "rep": r})

    for p in range(1, PLANE):
        for r in range(2):
            back_one(p, r).start()
    across = pltpu.make_async_remote_copy(
        src_ref=tot, dst_ref=r1.at[0, rep], send_sem=r1c.at[0], recv_sem=r1c.at[1],
        device_id={"rep": 1 - rep})
    across.start()
    r1[0, rep] = table
    pltpu.make_async_copy(r1.at[others], r1.at[others], r1r).wait()
    across.wait()

    lane = lax.broadcasted_iota(jnp.int32, (DEPTH, SLOTS), 1)
    sides = []
    for r in range(2):
        side = jnp.zeros((DEPTH, SLOTS), jnp.float32)
        for p in range(PLANE):
            side = jnp.where(lane // CL == p, r1[p, r], side)
        sides.append(side)
    for d in range(DEPTH):
        line = jnp.concatenate([s[d:d + 1] for s in sides], axis=1)
        s2[d] = line
        if d == 0:
            r2[0] = line
        else:
            pltpu.make_async_remote_copy(
                src_ref=s2.at[d], dst_ref=r2.at[d], send_sem=r2s, recv_sem=r2r,
                device_id={"shard": z_dev[(DEPTH - d) % DEPTH]}).start()
    rest = pl.ds(1, DEPTH - 1)
    pltpu.make_async_copy(r2.at[rest], r2.at[rest], r2r).wait()

    value = jnp.zeros((8, 128), jnp.float32)
    least = jnp.zeros((1, 2 * SLOTS), jnp.float32)
    for d in range(DEPTH):
        line = r2[d]
        least = jnp.minimum(least, line)
        for r in range(2):
            wide = jnp.broadcast_to(line[:, r * SLOTS:(r + 1) * SLOTS], (8, 128))
            found = jnp.take_along_axis(wide, doc_slot, axis=1)
            value = jnp.where((doc_z == d) & (doc_rep == r), found, value)
    out_ref[...] = jnp.where(jnp.min(least, axis=1, keepdims=True) < 0.0, -1.0, value)

    for d in ORDER:
        pltpu.make_async_copy(zs.at[d], zs.at[d], zss.at[d]).wait()
    for d in range(DEPTH):
        pltpu.make_async_copy(ps.at[d, others], ps.at[d, others], pss.at[d]).wait()
    pltpu.make_async_copy(r1.at[others], r1.at[others], r1s).wait()
    pltpu.make_async_copy(s2.at[rest], s2.at[rest], r2s).wait()


def packed_totals(embeddings, labels):
    dma = pltpu.SemaphoreType.DMA
    return pl.pallas_call(
        packed_kernel,
        out_shape=jax.ShapeDtypeStruct((8, 128), jnp.float32),
        in_specs=[pl.BlockSpec(memory_space=pl.ANY)] * 2,
        out_specs=pl.BlockSpec(memory_space=pltpu.VMEM),
        scratch_shapes=[
            pltpu.VMEM((DOCS_DEV, D), jnp.bfloat16),
            pltpu.VMEM((8, 128), jnp.int32),
            pltpu.VMEM((DEPTH, PACK, D), jnp.bfloat16),
            pltpu.VMEM((DEPTH, PACK, D), jnp.bfloat16),
            pltpu.VMEM((DEPTH, PLANE, CL, D), jnp.bfloat16),
            pltpu.VMEM((DEPTH, PLANE, CL, D), jnp.bfloat16),
            pltpu.VMEM((DEPTH * SLOTS, D), jnp.bfloat16),
            pltpu.VMEM((DEPTH, SLOTS), jnp.float32),
            pltpu.VMEM((PLANE, 2, DEPTH, SLOTS), jnp.float32),
            pltpu.VMEM((DEPTH, 1, 2 * SLOTS), jnp.float32),
            pltpu.VMEM((DEPTH, 1, 2 * SLOTS), jnp.float32),
            dma((2,)), dma((DEPTH,)), dma((DEPTH,)), dma((DEPTH,)), dma((DEPTH,)),
            dma, dma, dma((2,)), dma, dma,
        ],
        compiler_params=pltpu.CompilerParams(
            collective_id=1, has_side_effects=True, vmem_limit_bytes=60 * 1024 * 1024),
        name="packed_totals",
    )(embeddings, labels.reshape(8, 128))


def local(embeddings, labels):
    totals = packed_totals(embeddings, labels)
    totals = lax.cond(
        totals[0, 0] < 0.0, lambda: direct_totals(embeddings, labels), lambda: totals)
    return jnp.log1p(totals.reshape(DOCS_DEV))


def solution(mesh):
    return jax.shard_map(
        local,
        mesh=mesh,
        in_specs=(P("shard", None), P("shard")),
        out_specs=P("shard"),
        check_vma=False,
    )
```

```python
import functools
import jax
import jax.numpy as jnp
from jax import lax
from jax.experimental import pallas as pl
from jax.experimental.pallas import tpu as pltpu
from jax.sharding import PartitionSpec as P

SHARDS = 128
DOCS_DEV = 1024
D = 1024
CL = 8
GROUPS = 4
GROUP_Q = SHARDS // GROUPS
ROWS = GROUP_Q * CL

sharpness = 4.0
epsilon = 1e-06


def offset_of(q):
    k = q % 8
    dz = jnp.where(k % 2 == 1, (k + 1) // 2, (8 - k // 2) % 8)
    return (q // 32) % 4, (q // 8) % 4, dz


def q_of(dy, dx, dz):
    k = jnp.where(dz == 0, 0, jnp.where(dz <= 4, 2 * dz - 1, 2 * (8 - dz)))
    return dy * 32 + dx * 8 + k


def shift(s, q, sign):
    dy, dx, dz = offset_of(q)
    y = (s // 32 + 4 + sign * dy) % 4
    x = (s // 8 % 4 + 4 + sign * dx) % 4
    z = (s % 8 + 8 + sign * dz) % 8
    return y * 32 + x * 8 + z


def kernel(e_hbm, labels_ref, out_ref, e_ref, send, recv, unit, tot, ret, halves,
           load_sem, send_sem, recv_sem, back_send, back_recv, half_sem):
    me = lax.axis_index("shard")
    rep = lax.axis_index("rep")
    load = pltpu.make_async_copy(e_hbm, e_ref, load_sem)
    load.start()

    barrier = pltpu.get_barrier_semaphore()

    def greet(q, _):
        pl.semaphore_signal(barrier, inc=1, device_id={"shard": shift(me, q, -1)})
        return 0

    lax.fori_loop(1, SHARDS, greet, 0)
    pl.semaphore_signal(barrier, inc=1, device_id={"rep": 1 - rep})
    load.wait()

    labels = labels_ref[...]
    owner = labels // 16
    dy = (owner // 32 - me // 32 + 4) % 4
    dx = (owner // 8 % 4 - me // 8 % 4 + 4) % 4
    dz = (owner % 8 - me % 8 + 8) % 8
    doc_q = q_of(dy, dx, dz)
    doc_slot = jnp.where(labels % 16 // 8 == rep, doc_q * 8 + labels % 8, -1)

    def row_copy(q):
        return pltpu.make_async_remote_copy(
            src_ref=send.at[q], dst_ref=recv.at[q], send_sem=send_sem,
            recv_sem=recv_sem.at[q // GROUP_Q],
            device_id={"shard": shift(me, q, 1)})

    def back_copy(q):
        return pltpu.make_async_remote_copy(
            src_ref=tot.at[q // 16], dst_ref=ret.at[q], send_sem=back_send,
            recv_sem=back_recv, device_id={"shard": shift(me, q, -1)})

    def fill(g):
        ids = lax.broadcasted_iota(jnp.int32, (ROWS, 128), 0) + g * ROWS
        hits = [ids == doc_slot[j:j + 1, :] for j in range(8)]
        onehot = jnp.concatenate(
            [jnp.where(h, 1.0, 0.0).astype(jnp.bfloat16) for h in hits], axis=1)
        any_hit = functools.reduce(
            jnp.add, [jnp.where(h, 1.0, 0.0) for h in hits])
        present = jnp.sum(any_hit, axis=1, keepdims=True) > 0.0
        rows = jnp.dot(onehot, e_ref[...], preferred_element_type=jnp.float32)
        rows = jnp.where(present, rows, jnp.nan)
        rows = rows.reshape(GROUP_Q, CL, D).astype(jnp.bfloat16)
        send[g * GROUP_Q:(g + 1) * GROUP_Q] = rows
        if g == 0:
            recv[0] = rows[0]

    for g in range(GROUPS):
        fill(g)
        if g == 0:
            pl.semaphore_wait(barrier, SHARDS)

        def push(q, _):
            row_copy(q).start()
            return 0

        lax.fori_loop(1 if g == 0 else g * GROUP_Q, (g + 1) * GROUP_Q, push, 0)

    row_id = lax.broadcasted_iota(jnp.int32, (ROWS, ROWS), 0)
    col_id = lax.broadcasted_iota(jnp.int32, (ROWS, ROWS), 1)
    same = row_id % CL == col_id % CL
    same_off = same & (row_id != col_id)

    def weights(a, b, mask):
        gram = lax.dot_general(a, b, (((1,), (1,)), ((), ())),
                               preferred_element_type=jnp.float32)
        ok = mask & (gram == gram)
        w = jnp.where(ok, jnp.exp(sharpness * (gram - 1.0)), 0.0)
        return jnp.sum(w, axis=0, keepdims=True)

    totals = [jnp.zeros((1, ROWS), jnp.float32) for _ in range(GROUPS)]
    for g in range(GROUPS):
        lo = 1 if g == 0 else g * GROUP_Q
        block = pl.ds(lo, (g + 1) * GROUP_Q - lo)
        pltpu.make_async_copy(recv.at[block], recv.at[block], recv_sem.at[g]).wait()
        values = recv[g * GROUP_Q:(g + 1) * GROUP_Q].astype(jnp.float32).reshape(ROWS, D)
        scale = lax.rsqrt(jnp.sum(values * values, axis=1, keepdims=True) + epsilon)
        mine = (values * scale).astype(jnp.bfloat16)
        unit[g * ROWS:(g + 1) * ROWS] = mine
        totals[g] += weights(mine, mine, same_off)
        for h in range(g):
            other = unit[h * ROWS:(h + 1) * ROWS]
            totals[g] += weights(other, mine, same)
            totals[h] += weights(mine, other, same)

    for j in range(8):
        g, part = j // 2, j % 2
        tot[j] = totals[g][:, part * 128:(part + 1) * 128]
    ret[0] = tot[0]

    def push_back(q, _):
        back_copy(q).start()
        return 0

    lax.fori_loop(1, SHARDS, push_back, 0)
    everything = pl.ds(1, SHARDS - 1)
    pltpu.make_async_copy(ret.at[everything], ret.at[everything], back_recv).wait()

    got = ret[...].reshape(SHARDS, 128)
    q_id = lax.broadcasted_iota(jnp.int32, (SHARDS, 128), 0)
    lane = lax.broadcasted_iota(jnp.int32, (SHARDS, 128), 1)
    got = jnp.where(lane // CL == q_id % 16, got, 0.0).T
    halves[rep] = jnp.sum(got.reshape(16, CL, 128), axis=0)
    swap = pltpu.make_async_remote_copy(
        src_ref=halves.at[rep], dst_ref=halves.at[rep], send_sem=half_sem.at[0],
        recv_sem=half_sem.at[1], device_id={"rep": 1 - rep})
    swap.start()
    swap.wait()

    value = jnp.zeros((8, 128), jnp.float32)
    cluster = labels % 16
    for c in range(16):
        line = jnp.broadcast_to(halves[c // 8, c % 8:c % 8 + 1, :], (8, 128))
        value = jnp.where(cluster == c, jnp.take_along_axis(line, doc_q, axis=1), value)
    out_ref[...] = value

    pltpu.make_async_copy(send.at[everything], send.at[everything], send_sem).wait()
    pltpu.make_async_copy(ret.at[everything], ret.at[everything], back_send).wait()


def direct_totals(embeddings, labels):
    return pl.pallas_call(
        kernel,
        out_shape=jax.ShapeDtypeStruct((8, 128), jnp.float32),
        in_specs=[pl.BlockSpec(memory_space=pl.ANY), pl.BlockSpec(memory_space=pltpu.VMEM)],
        out_specs=pl.BlockSpec(memory_space=pltpu.VMEM),
        scratch_shapes=[
            pltpu.VMEM((DOCS_DEV, D), jnp.bfloat16),
            pltpu.VMEM((SHARDS, CL, D), jnp.bfloat16),
            pltpu.VMEM((SHARDS, CL, D), jnp.bfloat16),
            pltpu.VMEM((SHARDS * CL, D), jnp.bfloat16),
            pltpu.VMEM((8, 1, 128), jnp.float32),
            pltpu.VMEM((SHARDS, 1, 128), jnp.float32),
            pltpu.VMEM((2, 8, 128), jnp.float32),
            pltpu.SemaphoreType.DMA,
            pltpu.SemaphoreType.DMA,
            pltpu.SemaphoreType.DMA((GROUPS,)),
            pltpu.SemaphoreType.DMA,
            pltpu.SemaphoreType.DMA,
            pltpu.SemaphoreType.DMA((2,)),
        ],
        compiler_params=pltpu.CompilerParams(
            collective_id=0, has_side_effects=True, vmem_limit_bytes=48 * 1024 * 1024),
        name="cluster_totals",
    )(embeddings, labels.reshape(8, 128))


PLANE = 16
DEPTH = 8
SLOTS = PLANE * CL
CHIP_SLOTS = 2 * SLOTS
PACK = 168
LAST = PACK - 1
HALF = D // 2
PAIRS = ((1, 7), (2, 6), (3, 5), (4,))
ORDER = (1, 7, 2, 6, 3, 5, 4)


def prefix_rank(marks):
    i = lax.broadcasted_iota(jnp.int32, (CHIP_SLOTS, CHIP_SLOTS), 0)
    j = lax.broadcasted_iota(jnp.int32, (CHIP_SLOTS, CHIP_SLOTS), 1)
    before = jnp.where(i < j, 1.0, 0.0).astype(jnp.bfloat16)
    return jnp.dot(marks.astype(jnp.bfloat16), before, preferred_element_type=jnp.float32)


def mark_absent(rows, mark):
    column = jnp.broadcast_to(mark, (128, CHIP_SLOTS)).T
    first = jnp.where(column > 0.0, rows[:, :128], jnp.nan)
    return jnp.concatenate([first, rows[:, 128:]], axis=1)


def packed_kernel(e_hbm, labels_hbm, out_ref, flag_ref, e_ref, labels_ref, zs, zr, ps, pr, unit, tot,
                  r1, s2, r2, load_sem, zss, zrs, pss, prs, psc, prc, r1s, r1r, r1c, r2s, r2r):
    me = lax.axis_index("shard")
    rep = lax.axis_index("rep")
    y, x, z = me // 32, me // 8 % 4, me % 8
    z_dev = [y * 32 + x * 8 + (z + d) % 8 for d in range(DEPTH)]
    p_dev = [(y + p // 4) % 4 * 32 + (x + p % 4) % 4 * 8 + z for p in range(PLANE)]

    load_labels = pltpu.make_async_copy(labels_hbm, labels_ref, load_sem.at[1])
    load_labels.start()
    mine = pl.ds(pl.multiple_of(rep * HALF, HALF), HALF)
    load = pltpu.make_async_copy(e_hbm.at[:, mine], e_ref, load_sem.at[0])
    load.start()

    barrier = pltpu.get_barrier_semaphore()
    for d in range(1, DEPTH):
        pl.semaphore_signal(barrier, inc=1, device_id={"shard": z_dev[d]})
    for p in range(1, PLANE):
        for r in range(2):
            pl.semaphore_signal(barrier, inc=1, device_id={"shard": p_dev[p], "rep": r})
    pl.semaphore_signal(barrier, inc=1, device_id={"rep": 1 - rep})
    load_labels.wait()

    labels = labels_ref[...]
    owner = labels // 16
    doc_p = (owner // 32 - y + 4) % 4 * 4 + (owner // 8 % 4 - x + 4) % 4
    doc_z = (owner % 8 - z + 8) % 8
    doc_rep = labels % 16 // 8
    doc_slot = doc_p * CL + labels % 8
    doc_chip = doc_p * 16 + labels % 16
    doc_hi = doc_chip // 128 * DEPTH + doc_z
    doc_lo = doc_chip % 128

    def onehot(count, index):
        ids = lax.broadcasted_iota(jnp.int32, (count, 128), 0)
        return jnp.concatenate(
            [jnp.where(ids == index[j:j + 1, :], 1.0, 0.0).astype(jnp.bfloat16)
             for j in range(8)], axis=1)

    marks = lax.dot_general(onehot(2 * DEPTH, doc_hi), onehot(128, doc_lo),
                            (((1,), (1,)), ((), ())), preferred_element_type=jnp.float32)
    marks = jnp.concatenate([marks[:DEPTH], marks[DEPTH:]], axis=1)
    ranks = prefix_rank(marks)
    doc_rank = jnp.zeros((8, 128), jnp.float32)
    for h in range(2):
        for d in range(DEPTH):
            line = jnp.broadcast_to(ranks[d:d + 1, h * 128:(h + 1) * 128], (8, 128))
            doc_rank = jnp.where(
                doc_hi == h * DEPTH + d, jnp.take_along_axis(line, doc_lo, axis=1), doc_rank)
    doc_rank = doc_rank.astype(jnp.int32)
    row_id = lax.broadcasted_iota(jnp.int32, (PACK, CHIP_SLOTS), 0)

    def z_copy(d):
        return pltpu.make_async_remote_copy(
            src_ref=zs.at[d], dst_ref=zr.at[d], send_sem=zss.at[d], recv_sem=zrs.at[d],
            device_id={"shard": z_dev[d]})

    def forward(d):
        pltpu.make_async_remote_copy(
            src_ref=ps.at[d, 0, 1 - rep], dst_ref=pr.at[d, 0, rep], send_sem=psc.at[d],
            recv_sem=prc.at[d], device_id={"rep": 1 - rep}).start()
        for p in range(1, PLANE):
            for r in range(2):
                pltpu.make_async_remote_copy(
                    src_ref=ps.at[d, p, r], dst_ref=pr.at[d, p, rep], send_sem=pss.at[d],
                    recv_sem=prs.at[d], device_id={"shard": p_dev[p], "rep": r}).start()

    def spread(d, rows, mark):
        rows = mark_absent(rows, mark).reshape(PLANE, 2, CL, HALF).astype(jnp.bfloat16)
        ps[d] = rows
        pr[d, 0, rep] = ps[d, 0, rep]
        forward(d)

    def pack(group):
        select = jnp.concatenate(
            [onehot(PACK, jnp.where(doc_z == d, doc_rank, -1)) for d in group], axis=0)
        rows = jnp.dot(select, e_ref[...], preferred_element_type=jnp.float32)
        for i, d in enumerate(group):
            part = rows[i * PACK:(i + 1) * PACK]
            first = jnp.where(row_id == LAST, marks[d:d + 1], part[:, :CHIP_SLOTS])
            zs[d] = jnp.concatenate([first, part[:, CHIP_SLOTS:]], axis=1).astype(jnp.bfloat16)

    load.wait()
    pack(PAIRS[0])
    pl.semaphore_wait(barrier, DEPTH - 1 + 2 * PLANE - 1)
    for d in PAIRS[0]:
        z_copy(d).start()
    spread(0, jnp.dot(onehot(CHIP_SLOTS, jnp.where(doc_z == 0, doc_chip, -1)), e_ref[...],
                      preferred_element_type=jnp.float32), marks[:1])
    for group in PAIRS[1:]:
        pack(group)
        for d in group:
            z_copy(d).start()

    others = pl.ds(1, PLANE - 1)
    full = [jnp.zeros((1, CHIP_SLOTS), jnp.float32)]

    def expand(d):
        pltpu.make_async_copy(zr.at[d], zr.at[d], zrs.at[d]).wait()
        mark = zr[d, PACK - 8:PACK, :CHIP_SLOTS].astype(jnp.float32)[7:8]
        rank = prefix_rank(jnp.broadcast_to(mark, (16, CHIP_SLOTS)))[:1]
        full[0] = jnp.maximum(full[0], rank + mark)
        hit = (row_id == rank.astype(jnp.int32)) & (mark > 0.0) & (row_id < LAST)
        select = jnp.where(hit, 1.0, 0.0).astype(jnp.bfloat16)
        spread(d, lax.dot_general(select, zr[d], (((0,), (0,)), ((), ())),
                                  preferred_element_type=jnp.float32), mark)

    i = lax.broadcasted_iota(jnp.int32, (SLOTS, SLOTS), 0)
    j = lax.broadcasted_iota(jnp.int32, (SLOTS, SLOTS), 1)
    same = i % CL == j % CL
    same_off = same & (i != j)

    def weights(a, b, mask):
        gram = lax.dot_general(a, b, (((1,), (1,)), ((), ())),
                               preferred_element_type=jnp.float32)
        ok = mask & (gram == gram)
        w = jnp.where(ok, jnp.exp(sharpness * (gram - 1.0)), 0.0)
        return jnp.sum(w, axis=0, keepdims=True)

    totals = {}
    done = []

    def process(d):
        k = len(done)
        pltpu.make_async_copy(pr.at[d, others], pr.at[d, others], prs.at[d]).wait()
        pltpu.make_async_copy(pr.at[d, 0, 1 - rep], pr.at[d, 0, 1 - rep], prc.at[d]).wait()
        sides = [pr[d, :, f].astype(jnp.float32).reshape(SLOTS, HALF) for f in range(2)]
        square = jnp.sum(sides[0] * sides[0] + sides[1] * sides[1], axis=1, keepdims=True)
        scale = lax.rsqrt(square + epsilon)
        new = jnp.concatenate([(v * scale).astype(jnp.bfloat16) for v in sides], axis=1)
        unit[k * SLOTS:(k + 1) * SLOTS] = new
        total = weights(new, new, same_off)
        if k:
            before = unit[:k * SLOTS]
            total += weights(before, new, jnp.concatenate([same] * k, axis=0))
            rest = weights(new, before, jnp.concatenate([same] * k, axis=1))
            for n, e in enumerate(done):
                totals[e] += rest[:, n * SLOTS:(n + 1) * SLOTS]
        totals[d] = total
        done.append(d)

    expand(1)
    expand(7)
    process(0)
    expand(2)
    expand(6)
    process(1)
    process(7)
    expand(3)
    expand(5)
    process(2)
    process(6)
    expand(4)
    process(3)
    process(5)
    process(4)

    table = jnp.concatenate([totals[d] for d in range(DEPTH)], axis=0)
    table = jnp.where(jnp.max(full[0], axis=1, keepdims=True) > float(LAST), -1.0, table)
    tot[...] = table

    for p in range(1, PLANE):
        for r in range(2):
            pltpu.make_async_remote_copy(
                src_ref=tot, dst_ref=r1.at[(4 - p // 4) % 4 * 4 + (4 - p % 4) % 4, rep],
                send_sem=r1s, recv_sem=r1r, device_id={"shard": p_dev[p], "rep": r}).start()
    across = pltpu.make_async_remote_copy(
        src_ref=tot, dst_ref=r1.at[0, rep], send_sem=r1c.at[0], recv_sem=r1c.at[1],
        device_id={"rep": 1 - rep})
    across.start()
    r1[0, rep] = table
    pltpu.make_async_copy(r1.at[others], r1.at[others], r1r).wait()
    across.wait()

    lane = lax.broadcasted_iota(jnp.int32, (DEPTH, SLOTS), 1)
    sides = []
    for r in range(2):
        side = jnp.zeros((DEPTH, SLOTS), jnp.float32)
        for p in range(PLANE):
            side = jnp.where(lane // CL == p, r1[p, r], side)
        sides.append(side)
    for d in range(DEPTH):
        line = jnp.concatenate([s[d:d + 1] for s in sides], axis=1)
        s2[d] = line
        if d == 0:
            r2[0] = line
        else:
            pltpu.make_async_remote_copy(
                src_ref=s2.at[d], dst_ref=r2.at[d], send_sem=r2s, recv_sem=r2r,
                device_id={"shard": z_dev[(DEPTH - d) % DEPTH]}).start()
    rest = pl.ds(1, DEPTH - 1)
    pltpu.make_async_copy(r2.at[rest], r2.at[rest], r2r).wait()

    value = jnp.zeros((8, 128), jnp.float32)
    least = jnp.zeros((1, 2 * SLOTS), jnp.float32)
    for d in range(DEPTH):
        line = r2[d]
        least = jnp.minimum(least, line)
        for r in range(2):
            wide = jnp.broadcast_to(line[:, r * SLOTS:(r + 1) * SLOTS], (8, 128))
            found = jnp.take_along_axis(wide, doc_slot, axis=1)
            value = jnp.where((doc_z == d) & (doc_rep == r), found, value)
    out_ref[...] = value
    flag_ref[0] = jnp.where(jnp.min(least) < 0.0, 1, 0).astype(jnp.int32)

    for d in ORDER:
        pltpu.make_async_copy(zs.at[d], zs.at[d], zss.at[d]).wait()
    for d in range(DEPTH):
        pltpu.make_async_copy(ps.at[d, others], ps.at[d, others], pss.at[d]).wait()
        pltpu.make_async_copy(ps.at[d, 0, 1 - rep], ps.at[d, 0, 1 - rep], psc.at[d]).wait()
    pltpu.make_async_copy(r1.at[others], r1.at[others], r1s).wait()
    pltpu.make_async_copy(s2.at[rest], s2.at[rest], r2s).wait()


def packed_totals(embeddings, labels):
    dma = pltpu.SemaphoreType.DMA
    return pl.pallas_call(
        packed_kernel,
        out_shape=(jax.ShapeDtypeStruct((8, 128), jnp.float32),
                   jax.ShapeDtypeStruct((1,), jnp.int32)),
        in_specs=[pl.BlockSpec(memory_space=pl.ANY)] * 2,
        out_specs=(pl.BlockSpec(memory_space=pltpu.VMEM), pl.BlockSpec(memory_space=pltpu.SMEM)),
        scratch_shapes=[
            pltpu.VMEM((DOCS_DEV, HALF), jnp.bfloat16),
            pltpu.VMEM((8, 128), jnp.int32),
            pltpu.VMEM((DEPTH, PACK, HALF), jnp.bfloat16),
            pltpu.VMEM((DEPTH, PACK, HALF), jnp.bfloat16),
            pltpu.VMEM((DEPTH, PLANE, 2, CL, HALF), jnp.bfloat16),
            pltpu.VMEM((DEPTH, PLANE, 2, CL, HALF), jnp.bfloat16),
            pltpu.VMEM((DEPTH * SLOTS, D), jnp.bfloat16),
            pltpu.VMEM((DEPTH, SLOTS), jnp.float32),
            pltpu.VMEM((PLANE, 2, DEPTH, SLOTS), jnp.float32),
            pltpu.VMEM((DEPTH, 1, 2 * SLOTS), jnp.float32),
            pltpu.VMEM((DEPTH, 1, 2 * SLOTS), jnp.float32),
            dma((2,)), dma((DEPTH,)), dma((DEPTH,)), dma((DEPTH,)), dma((DEPTH,)),
            dma((DEPTH,)), dma((DEPTH,)), dma, dma, dma((2,)), dma, dma,
        ],
        compiler_params=pltpu.CompilerParams(
            collective_id=1, has_side_effects=True, vmem_limit_bytes=60 * 1024 * 1024),
        name="packed_totals",
    )(embeddings, labels.reshape(8, 128))


def local(embeddings, labels):
    totals, overflow = packed_totals(embeddings, labels)
    totals = lax.cond(
        overflow[0] > 0, lambda: direct_totals(embeddings, labels), lambda: totals)
    return jnp.log1p(totals.reshape(DOCS_DEV))


def solution(mesh):
    return jax.shard_map(
        local,
        mesh=mesh,
        in_specs=(P("shard", None), P("shard")),
        out_specs=P("shard"),
        check_vma=False,
    )
```

```python
import functools
import jax
import jax.numpy as jnp
from jax import lax
from jax.experimental import pallas as pl
from jax.experimental.pallas import tpu as pltpu
from jax.sharding import PartitionSpec as P

SHARDS = 128
DOCS_DEV = 1024
D = 1024
CL = 8
GROUPS = 4
GROUP_Q = SHARDS // GROUPS
ROWS = GROUP_Q * CL

sharpness = 4.0
epsilon = 1e-06


def offset_of(q):
    k = q % 8
    dz = jnp.where(k % 2 == 1, (k + 1) // 2, (8 - k // 2) % 8)
    return (q // 32) % 4, (q // 8) % 4, dz


def q_of(dy, dx, dz):
    k = jnp.where(dz == 0, 0, jnp.where(dz <= 4, 2 * dz - 1, 2 * (8 - dz)))
    return dy * 32 + dx * 8 + k


def shift(s, q, sign):
    dy, dx, dz = offset_of(q)
    y = (s // 32 + 4 + sign * dy) % 4
    x = (s // 8 % 4 + 4 + sign * dx) % 4
    z = (s % 8 + 8 + sign * dz) % 8
    return y * 32 + x * 8 + z


def kernel(e_hbm, labels_ref, out_ref, e_ref, send, recv, unit, tot, ret, halves,
           load_sem, send_sem, recv_sem, back_send, back_recv, half_sem):
    me = lax.axis_index("shard")
    rep = lax.axis_index("rep")
    load = pltpu.make_async_copy(e_hbm, e_ref, load_sem)
    load.start()

    barrier = pltpu.get_barrier_semaphore()

    def greet(q, _):
        pl.semaphore_signal(barrier, inc=1, device_id={"shard": shift(me, q, -1)})
        return 0

    lax.fori_loop(1, SHARDS, greet, 0)
    pl.semaphore_signal(barrier, inc=1, device_id={"rep": 1 - rep})
    load.wait()

    labels = labels_ref[...]
    owner = labels // 16
    dy = (owner // 32 - me // 32 + 4) % 4
    dx = (owner // 8 % 4 - me // 8 % 4 + 4) % 4
    dz = (owner % 8 - me % 8 + 8) % 8
    doc_q = q_of(dy, dx, dz)
    doc_slot = jnp.where(labels % 16 // 8 == rep, doc_q * 8 + labels % 8, -1)

    def row_copy(q):
        return pltpu.make_async_remote_copy(
            src_ref=send.at[q], dst_ref=recv.at[q], send_sem=send_sem,
            recv_sem=recv_sem.at[q // GROUP_Q],
            device_id={"shard": shift(me, q, 1)})

    def back_copy(q):
        return pltpu.make_async_remote_copy(
            src_ref=tot.at[q // 16], dst_ref=ret.at[q], send_sem=back_send,
            recv_sem=back_recv, device_id={"shard": shift(me, q, -1)})

    def fill(g):
        ids = lax.broadcasted_iota(jnp.int32, (ROWS, 128), 0) + g * ROWS
        hits = [ids == doc_slot[j:j + 1, :] for j in range(8)]
        onehot = jnp.concatenate(
            [jnp.where(h, 1.0, 0.0).astype(jnp.bfloat16) for h in hits], axis=1)
        any_hit = functools.reduce(
            jnp.add, [jnp.where(h, 1.0, 0.0) for h in hits])
        present = jnp.sum(any_hit, axis=1, keepdims=True) > 0.0
        rows = jnp.dot(onehot, e_ref[...], preferred_element_type=jnp.float32)
        rows = jnp.where(present, rows, jnp.nan)
        rows = rows.reshape(GROUP_Q, CL, D).astype(jnp.bfloat16)
        send[g * GROUP_Q:(g + 1) * GROUP_Q] = rows
        if g == 0:
            recv[0] = rows[0]

    for g in range(GROUPS):
        fill(g)
        if g == 0:
            pl.semaphore_wait(barrier, SHARDS)

        def push(q, _):
            row_copy(q).start()
            return 0

        lax.fori_loop(1 if g == 0 else g * GROUP_Q, (g + 1) * GROUP_Q, push, 0)

    row_id = lax.broadcasted_iota(jnp.int32, (ROWS, ROWS), 0)
    col_id = lax.broadcasted_iota(jnp.int32, (ROWS, ROWS), 1)
    same = row_id % CL == col_id % CL
    same_off = same & (row_id != col_id)

    def weights(a, b, mask):
        gram = lax.dot_general(a, b, (((1,), (1,)), ((), ())),
                               preferred_element_type=jnp.float32)
        ok = mask & (gram == gram)
        w = jnp.where(ok, jnp.exp(sharpness * (gram - 1.0)), 0.0)
        return jnp.sum(w, axis=0, keepdims=True)

    totals = [jnp.zeros((1, ROWS), jnp.float32) for _ in range(GROUPS)]
    for g in range(GROUPS):
        lo = 1 if g == 0 else g * GROUP_Q
        block = pl.ds(lo, (g + 1) * GROUP_Q - lo)
        pltpu.make_async_copy(recv.at[block], recv.at[block], recv_sem.at[g]).wait()
        values = recv[g * GROUP_Q:(g + 1) * GROUP_Q].astype(jnp.float32).reshape(ROWS, D)
        scale = lax.rsqrt(jnp.sum(values * values, axis=1, keepdims=True) + epsilon)
        mine = (values * scale).astype(jnp.bfloat16)
        unit[g * ROWS:(g + 1) * ROWS] = mine
        totals[g] += weights(mine, mine, same_off)
        for h in range(g):
            other = unit[h * ROWS:(h + 1) * ROWS]
            totals[g] += weights(other, mine, same)
            totals[h] += weights(mine, other, same)

    for j in range(8):
        g, part = j // 2, j % 2
        tot[j] = totals[g][:, part * 128:(part + 1) * 128]
    ret[0] = tot[0]

    def push_back(q, _):
        back_copy(q).start()
        return 0

    lax.fori_loop(1, SHARDS, push_back, 0)
    everything = pl.ds(1, SHARDS - 1)
    pltpu.make_async_copy(ret.at[everything], ret.at[everything], back_recv).wait()

    got = ret[...].reshape(SHARDS, 128)
    q_id = lax.broadcasted_iota(jnp.int32, (SHARDS, 128), 0)
    lane = lax.broadcasted_iota(jnp.int32, (SHARDS, 128), 1)
    got = jnp.where(lane // CL == q_id % 16, got, 0.0).T
    halves[rep] = jnp.sum(got.reshape(16, CL, 128), axis=0)
    swap = pltpu.make_async_remote_copy(
        src_ref=halves.at[rep], dst_ref=halves.at[rep], send_sem=half_sem.at[0],
        recv_sem=half_sem.at[1], device_id={"rep": 1 - rep})
    swap.start()
    swap.wait()

    value = jnp.zeros((8, 128), jnp.float32)
    cluster = labels % 16
    for c in range(16):
        line = jnp.broadcast_to(halves[c // 8, c % 8:c % 8 + 1, :], (8, 128))
        value = jnp.where(cluster == c, jnp.take_along_axis(line, doc_q, axis=1), value)
    out_ref[...] = value

    pltpu.make_async_copy(send.at[everything], send.at[everything], send_sem).wait()
    pltpu.make_async_copy(ret.at[everything], ret.at[everything], back_send).wait()


def direct_totals(embeddings, labels):
    return pl.pallas_call(
        kernel,
        out_shape=jax.ShapeDtypeStruct((8, 128), jnp.float32),
        in_specs=[pl.BlockSpec(memory_space=pl.ANY), pl.BlockSpec(memory_space=pltpu.VMEM)],
        out_specs=pl.BlockSpec(memory_space=pltpu.VMEM),
        scratch_shapes=[
            pltpu.VMEM((DOCS_DEV, D), jnp.bfloat16),
            pltpu.VMEM((SHARDS, CL, D), jnp.bfloat16),
            pltpu.VMEM((SHARDS, CL, D), jnp.bfloat16),
            pltpu.VMEM((SHARDS * CL, D), jnp.bfloat16),
            pltpu.VMEM((8, 1, 128), jnp.float32),
            pltpu.VMEM((SHARDS, 1, 128), jnp.float32),
            pltpu.VMEM((2, 8, 128), jnp.float32),
            pltpu.SemaphoreType.DMA,
            pltpu.SemaphoreType.DMA,
            pltpu.SemaphoreType.DMA((GROUPS,)),
            pltpu.SemaphoreType.DMA,
            pltpu.SemaphoreType.DMA,
            pltpu.SemaphoreType.DMA((2,)),
        ],
        compiler_params=pltpu.CompilerParams(
            collective_id=0, has_side_effects=True, vmem_limit_bytes=48 * 1024 * 1024),
        name="cluster_totals",
    )(embeddings, labels.reshape(8, 128))


PLANE = 16
DEPTH = 8
SLOTS = PLANE * CL
CHIP_SLOTS = 2 * SLOTS
PACK = 160
HALF = D // 2
PAIRS = ((1, 7), (2, 6), (3, 5), (4,))
ORDER = (1, 7, 2, 6, 3, 5, 4)
FAR_Z = (4, 3, 5, 2, 6, 1, 7)
FAR_PARTS = ((10, 9, 11, 8), (6, 5, 7, 4), (14, 13, 15, 12), (2, 1, 3, 0))
FAR_PLANE = (10, 9, 11, 6, 14, 8, 2, 5, 7, 13, 15, 4, 12, 1, 3)


def prefix_rank(marks):
    i = lax.broadcasted_iota(jnp.int32, (CHIP_SLOTS, CHIP_SLOTS), 0)
    j = lax.broadcasted_iota(jnp.int32, (CHIP_SLOTS, CHIP_SLOTS), 1)
    before = jnp.where(i < j, 1.0, 0.0).astype(jnp.bfloat16)
    return jnp.dot(marks.astype(jnp.bfloat16), before, preferred_element_type=jnp.float32)


def mark_column(mark):
    return jnp.broadcast_to(mark, (128, CHIP_SLOTS)).T


def mark_absent(rows, column):
    first = jnp.where(column > 0.0, rows[:, :128], jnp.nan)
    return jnp.concatenate([first, rows[:, 128:]], axis=1)


def packed_kernel(e_hbm, labels_hbm, out_ref, flag_ref, e_ref, labels_ref, zs, zr, ms, mr, ps, pr, unit, tot,
                  r1, s2, r2, load_sem, mss, mrs, zss, zrs, pss, prs, psc, prc, r1s, r1r, r1c, r2s, r2r):
    me = lax.axis_index("shard")
    rep = lax.axis_index("rep")
    y, x, z = me // 32, me // 8 % 4, me % 8
    z_dev = [y * 32 + x * 8 + (z + d) % 8 for d in range(DEPTH)]
    p_dev = [(y + p // 4) % 4 * 32 + (x + p % 4) % 4 * 8 + z for p in range(PLANE)]

    load_labels = pltpu.make_async_copy(labels_hbm, labels_ref, load_sem.at[1])
    load_labels.start()
    mine = pl.ds(pl.multiple_of(rep * HALF, HALF), HALF)
    load = pltpu.make_async_copy(e_hbm.at[:, mine], e_ref, load_sem.at[0])
    load.start()

    barrier = pltpu.get_barrier_semaphore()
    for target in [z_dev[d] for d in FAR_Z] + [p_dev[p] for p in FAR_PLANE]:
        for r in range(2):
            pl.semaphore_signal(barrier, inc=1, device_id={"shard": target, "rep": r})
    pl.semaphore_signal(barrier, inc=1, device_id={"rep": 1 - rep})
    load_labels.wait()

    labels = labels_ref[...]
    owner = labels // 16
    doc_p = (owner // 32 - y + 4) % 4 * 4 + (owner // 8 % 4 - x + 4) % 4
    doc_z = (owner % 8 - z + 8) % 8
    doc_rep = labels % 16 // 8
    doc_slot = doc_p * CL + labels % 8
    doc_chip = doc_p * 16 + labels % 16
    doc_hi = doc_chip // 128 * DEPTH + doc_z
    doc_lo = doc_chip % 128

    def onehot(count, index):
        ids = lax.broadcasted_iota(jnp.int32, (count, 128), 0)
        return jnp.concatenate(
            [jnp.where(ids == index[j:j + 1, :], 1.0, 0.0).astype(jnp.bfloat16)
             for j in range(8)], axis=1)

    marks = lax.dot_general(onehot(2 * DEPTH, doc_hi), onehot(128, doc_lo),
                            (((1,), (1,)), ((), ())), preferred_element_type=jnp.float32)
    marks = jnp.concatenate([marks[:DEPTH], marks[DEPTH:]], axis=1)
    ranks = prefix_rank(marks)
    doc_rank = jnp.zeros((8, 128), jnp.float32)
    for h in range(2):
        for d in range(DEPTH):
            line = jnp.broadcast_to(ranks[d:d + 1, h * 128:(h + 1) * 128], (8, 128))
            doc_rank = jnp.where(
                doc_hi == h * DEPTH + d, jnp.take_along_axis(line, doc_lo, axis=1), doc_rank)
    doc_rank = doc_rank.astype(jnp.int32)
    row_id = lax.broadcasted_iota(jnp.int32, (PACK, CHIP_SLOTS), 0)
    for d in range(1, DEPTH):
        ms[d] = marks[d:d + 1]

    def mark_copy(d):
        return pltpu.make_async_remote_copy(
            src_ref=ms.at[d], dst_ref=mr.at[d], send_sem=mss, recv_sem=mrs,
            device_id={"shard": z_dev[d]})

    def z_copy(d):
        return pltpu.make_async_remote_copy(
            src_ref=zs.at[d], dst_ref=zr.at[d], send_sem=zss.at[d], recv_sem=zrs.at[d],
            device_id={"shard": z_dev[d]})

    def spread(d, part, rows, column):
        low = part[-1] * 16
        rows = mark_absent(rows, column[low:low + 64])
        ps[d, part[-1]:part[-1] + 4] = rows.reshape(4, 2, CL, HALF).astype(jnp.bfloat16)
        for p in part:
            if p == 0:
                pltpu.make_async_remote_copy(
                    src_ref=ps.at[d, 0, 1 - rep], dst_ref=pr.at[d, 0, rep], send_sem=psc.at[d],
                    recv_sem=prc.at[d], device_id={"rep": 1 - rep}).start()
                pr[d, 0, rep] = ps[d, 0, rep]
                continue
            for r in range(2):
                pltpu.make_async_remote_copy(
                    src_ref=ps.at[d, p, r], dst_ref=pr.at[d, p, rep], send_sem=pss.at[d],
                    recv_sem=prs.at[d], device_id={"shard": p_dev[p], "rep": r}).start()

    def pack(group):
        select = jnp.concatenate(
            [onehot(PACK, jnp.where(doc_z == d, doc_rank, -1)) for d in group], axis=0)
        rows = jnp.dot(select, e_ref[...], preferred_element_type=jnp.float32)
        for i, d in enumerate(group):
            zs[d] = rows[i * PACK:(i + 1) * PACK].astype(jnp.bfloat16)

    load.wait()
    pack(PAIRS[0])
    pl.semaphore_wait(barrier, 2 * (DEPTH - 1) + 2 * (PLANE - 1) + 1)
    for d in FAR_Z:
        mark_copy(d).start()
    for d in PAIRS[0]:
        z_copy(d).start()
    rows = jnp.dot(onehot(CHIP_SLOTS, jnp.where(doc_z == 0, doc_chip, -1)), e_ref[...],
                   preferred_element_type=jnp.float32)
    column = mark_column(marks[:1])
    for part in FAR_PARTS:
        spread(0, part, rows[part[-1] * 16:part[-1] * 16 + 64], column)
    for group in PAIRS[1:]:
        pack(group)
        for d in group:
            z_copy(d).start()

    others = pl.ds(1, PLANE - 1)
    around = pl.ds(1, DEPTH - 1)
    pltpu.make_async_copy(mr.at[around], mr.at[around], mrs).wait()
    there = jnp.concatenate([jnp.zeros((1, CHIP_SLOTS), jnp.float32)]
                            + [mr[d] for d in range(1, DEPTH)], axis=0)
    ranks = prefix_rank(there)
    full = jnp.max(ranks + there)
    ranks = jnp.where(there > 0.0, ranks, -1.0).astype(jnp.int32)

    def expand(d):
        select = jnp.where(row_id == ranks[d:d + 1], 1.0, 0.0).astype(jnp.bfloat16)
        column = mark_column(there[d:d + 1])
        pltpu.make_async_copy(zr.at[d], zr.at[d], zrs.at[d]).wait()
        rows = lax.dot_general(select, zr[d], (((0,), (0,)), ((), ())),
                               preferred_element_type=jnp.float32)
        for part in FAR_PARTS:
            spread(d, part, rows[part[-1] * 16:part[-1] * 16 + 64], column)

    i = lax.broadcasted_iota(jnp.int32, (SLOTS, SLOTS), 0)
    j = lax.broadcasted_iota(jnp.int32, (SLOTS, SLOTS), 1)
    same = i % CL == j % CL
    same_off = same & (i != j)

    def weights(a, b, mask):
        gram = lax.dot_general(a, b, (((1,), (1,)), ((), ())),
                               preferred_element_type=jnp.float32)
        ok = mask & (gram == gram)
        w = jnp.where(ok, jnp.exp(sharpness * (gram - 1.0)), 0.0)
        return jnp.sum(w, axis=0, keepdims=True)

    totals = {}
    done = []

    def process(d):
        k = len(done)
        pltpu.make_async_copy(pr.at[d, others], pr.at[d, others], prs.at[d]).wait()
        pltpu.make_async_copy(pr.at[d, 0, 1 - rep], pr.at[d, 0, 1 - rep], prc.at[d]).wait()
        sides = [pr[d, :, f].astype(jnp.float32).reshape(SLOTS, HALF) for f in range(2)]
        square = jnp.sum(sides[0] * sides[0] + sides[1] * sides[1], axis=1, keepdims=True)
        scale = lax.rsqrt(square + epsilon)
        new = jnp.concatenate([(v * scale).astype(jnp.bfloat16) for v in sides], axis=1)
        unit[k * SLOTS:(k + 1) * SLOTS] = new
        total = weights(new, new, same_off)
        if k:
            before = unit[:k * SLOTS]
            total += weights(before, new, jnp.concatenate([same] * k, axis=0))
            rest = weights(new, before, jnp.concatenate([same] * k, axis=1))
            for n, e in enumerate(done):
                totals[e] += rest[:, n * SLOTS:(n + 1) * SLOTS]
        totals[d] = total
        done.append(d)

    expand(1)
    expand(7)
    process(0)
    expand(2)
    expand(6)
    process(1)
    process(7)
    expand(3)
    expand(5)
    process(2)
    process(6)
    expand(4)
    process(3)
    process(5)
    process(4)

    table = jnp.concatenate([totals[d] for d in range(DEPTH)], axis=0)
    table = jnp.where(full > float(PACK), -1.0, table)
    for d in range(DEPTH):
        tot[d] = table[d:d + 1]

    for d in FAR_Z:
        for r in range(2):
            pltpu.make_async_remote_copy(
                src_ref=tot.at[d], dst_ref=r1.at[d, rep], send_sem=r1s, recv_sem=r1r,
                device_id={"shard": z_dev[(DEPTH - d) % DEPTH], "rep": r}).start()
    across = pltpu.make_async_remote_copy(
        src_ref=tot.at[0], dst_ref=r1.at[0, rep], send_sem=r1c.at[0], recv_sem=r1c.at[1],
        device_id={"rep": 1 - rep})
    across.start()
    r1[0, rep] = table[:1]
    pltpu.make_async_copy(r1.at[around], r1.at[around], r1r).wait()
    across.wait()

    lane = lax.broadcasted_iota(jnp.int32, (8, SLOTS), 1)
    base = lax.broadcasted_iota(jnp.int32, (8, SLOTS), 0) * CL + lane % CL
    blocks = [jnp.zeros((8, SLOTS), jnp.float32) for _ in range(2)]
    for n in range(2 * DEPTH):
        line = jnp.broadcast_to(r1[n // 2, n % 2], (8, SLOTS))
        for h in range(2):
            moved = jnp.take_along_axis(line, base + h * 64, axis=1)
            blocks[h] = jnp.where(lane // CL == n, moved, blocks[h])
    for p in (0,) + FAR_PLANE:
        s2[p] = blocks[p // 8][p % 8:p % 8 + 1]
    r2[0] = blocks[0][:1]
    for p in FAR_PLANE:
        pltpu.make_async_remote_copy(
            src_ref=s2.at[p], dst_ref=r2.at[p], send_sem=r2s, recv_sem=r2r,
            device_id={"shard": p_dev[(4 - p // 4) % 4 * 4 + (4 - p % 4) % 4]}).start()
    pltpu.make_async_copy(r2.at[others], r2.at[others], r2r).wait()

    value = jnp.zeros((8, 128), jnp.float32)
    least = jnp.zeros((1, SLOTS), jnp.float32)
    doc_lane = doc_z * 16 + labels % 16
    for p in range(PLANE):
        line = r2[p]
        least = jnp.minimum(least, line)
        found = jnp.take_along_axis(jnp.broadcast_to(line, (8, 128)), doc_lane, axis=1)
        value = jnp.where(doc_p == p, found, value)
    out_ref[...] = value
    flag_ref[0] = jnp.where(jnp.min(least) < 0.0, 1, 0).astype(jnp.int32)

    for d in ORDER:
        pltpu.make_async_copy(zs.at[d], zs.at[d], zss.at[d]).wait()
    for d in range(DEPTH):
        pltpu.make_async_copy(ps.at[d, others], ps.at[d, others], pss.at[d]).wait()
        pltpu.make_async_copy(ps.at[d, 0, 1 - rep], ps.at[d, 0, 1 - rep], psc.at[d]).wait()
    pltpu.make_async_copy(ms.at[around], ms.at[around], mss).wait()
    pltpu.make_async_copy(r1.at[around], r1.at[around], r1s).wait()
    pltpu.make_async_copy(s2.at[others], s2.at[others], r2s).wait()


def packed_totals(embeddings, labels):
    dma = pltpu.SemaphoreType.DMA
    return pl.pallas_call(
        packed_kernel,
        out_shape=(jax.ShapeDtypeStruct((8, 128), jnp.float32),
                   jax.ShapeDtypeStruct((1,), jnp.int32)),
        in_specs=[pl.BlockSpec(memory_space=pl.ANY)] * 2,
        out_specs=(pl.BlockSpec(memory_space=pltpu.VMEM), pl.BlockSpec(memory_space=pltpu.SMEM)),
        scratch_shapes=[
            pltpu.VMEM((DOCS_DEV, HALF), jnp.bfloat16),
            pltpu.VMEM((8, 128), jnp.int32),
            pltpu.VMEM((DEPTH, PACK, HALF), jnp.bfloat16),
            pltpu.VMEM((DEPTH, PACK, HALF), jnp.bfloat16),
            pltpu.VMEM((DEPTH, 1, CHIP_SLOTS), jnp.float32),
            pltpu.VMEM((DEPTH, 1, CHIP_SLOTS), jnp.float32),
            pltpu.VMEM((DEPTH, PLANE, 2, CL, HALF), jnp.bfloat16),
            pltpu.VMEM((DEPTH, PLANE, 2, CL, HALF), jnp.bfloat16),
            pltpu.VMEM((DEPTH * SLOTS, D), jnp.bfloat16),
            pltpu.VMEM((DEPTH, 1, SLOTS), jnp.float32),
            pltpu.VMEM((DEPTH, 2, 1, SLOTS), jnp.float32),
            pltpu.VMEM((PLANE, 1, SLOTS), jnp.float32),
            pltpu.VMEM((PLANE, 1, SLOTS), jnp.float32),
            dma((2,)), dma, dma, dma((DEPTH,)), dma((DEPTH,)), dma((DEPTH,)), dma((DEPTH,)),
            dma((DEPTH,)), dma((DEPTH,)), dma, dma, dma((2,)), dma, dma,
        ],
        compiler_params=pltpu.CompilerParams(
            collective_id=1, has_side_effects=True, vmem_limit_bytes=60 * 1024 * 1024),
        name="packed_totals",
    )(embeddings, labels.reshape(8, 128))


def local(embeddings, labels):
    totals, overflow = packed_totals(embeddings, labels)
    totals = lax.cond(
        overflow[0] > 0, lambda: direct_totals(embeddings, labels), lambda: totals)
    return jnp.log1p(totals.reshape(DOCS_DEV))


def solution(mesh):
    return jax.shard_map(
        local,
        mesh=mesh,
        in_specs=(P("shard", None), P("shard")),
        out_specs=P("shard"),
        check_vma=False,
    )
```

```python
import functools
import jax
import jax.numpy as jnp
from jax import lax
from jax.experimental import pallas as pl
from jax.experimental.pallas import tpu as pltpu
from jax.sharding import PartitionSpec as P

SHARDS = 128
DOCS_DEV = 1024
D = 1024
CL = 8
GROUPS = 4
GROUP_Q = SHARDS // GROUPS
ROWS = GROUP_Q * CL

sharpness = 4.0
epsilon = 1e-06


def offset_of(q):
    k = q % 8
    dz = jnp.where(k % 2 == 1, (k + 1) // 2, (8 - k // 2) % 8)
    return (q // 32) % 4, (q // 8) % 4, dz


def q_of(dy, dx, dz):
    k = jnp.where(dz == 0, 0, jnp.where(dz <= 4, 2 * dz - 1, 2 * (8 - dz)))
    return dy * 32 + dx * 8 + k


def shift(s, q, sign):
    dy, dx, dz = offset_of(q)
    y = (s // 32 + 4 + sign * dy) % 4
    x = (s // 8 % 4 + 4 + sign * dx) % 4
    z = (s % 8 + 8 + sign * dz) % 8
    return y * 32 + x * 8 + z


def kernel(e_hbm, labels_ref, out_ref, e_ref, send, recv, unit, tot, ret, halves,
           load_sem, send_sem, recv_sem, back_send, back_recv, half_sem):
    me = lax.axis_index("shard")
    rep = lax.axis_index("rep")
    load = pltpu.make_async_copy(e_hbm, e_ref, load_sem)
    load.start()

    barrier = pltpu.get_barrier_semaphore()

    def greet(q, _):
        pl.semaphore_signal(barrier, inc=1, device_id={"shard": shift(me, q, -1)})
        return 0

    lax.fori_loop(1, SHARDS, greet, 0)
    pl.semaphore_signal(barrier, inc=1, device_id={"rep": 1 - rep})
    load.wait()

    labels = labels_ref[...]
    owner = labels // 16
    dy = (owner // 32 - me // 32 + 4) % 4
    dx = (owner // 8 % 4 - me // 8 % 4 + 4) % 4
    dz = (owner % 8 - me % 8 + 8) % 8
    doc_q = q_of(dy, dx, dz)
    doc_slot = jnp.where(labels % 16 // 8 == rep, doc_q * 8 + labels % 8, -1)

    def row_copy(q):
        return pltpu.make_async_remote_copy(
            src_ref=send.at[q], dst_ref=recv.at[q], send_sem=send_sem,
            recv_sem=recv_sem.at[q // GROUP_Q],
            device_id={"shard": shift(me, q, 1)})

    def back_copy(q):
        return pltpu.make_async_remote_copy(
            src_ref=tot.at[q // 16], dst_ref=ret.at[q], send_sem=back_send,
            recv_sem=back_recv, device_id={"shard": shift(me, q, -1)})

    def fill(g):
        ids = lax.broadcasted_iota(jnp.int32, (ROWS, 128), 0) + g * ROWS
        hits = [ids == doc_slot[j:j + 1, :] for j in range(8)]
        onehot = jnp.concatenate(
            [jnp.where(h, 1.0, 0.0).astype(jnp.bfloat16) for h in hits], axis=1)
        any_hit = functools.reduce(
            jnp.add, [jnp.where(h, 1.0, 0.0) for h in hits])
        present = jnp.sum(any_hit, axis=1, keepdims=True) > 0.0
        rows = jnp.dot(onehot, e_ref[...], preferred_element_type=jnp.float32)
        rows = jnp.where(present, rows, jnp.nan)
        rows = rows.reshape(GROUP_Q, CL, D).astype(jnp.bfloat16)
        send[g * GROUP_Q:(g + 1) * GROUP_Q] = rows
        if g == 0:
            recv[0] = rows[0]

    for g in range(GROUPS):
        fill(g)
        if g == 0:
            pl.semaphore_wait(barrier, SHARDS)

        def push(q, _):
            row_copy(q).start()
            return 0

        lax.fori_loop(1 if g == 0 else g * GROUP_Q, (g + 1) * GROUP_Q, push, 0)

    row_id = lax.broadcasted_iota(jnp.int32, (ROWS, ROWS), 0)
    col_id = lax.broadcasted_iota(jnp.int32, (ROWS, ROWS), 1)
    same = row_id % CL == col_id % CL
    same_off = same & (row_id != col_id)

    def weights(a, b, mask):
        gram = lax.dot_general(a, b, (((1,), (1,)), ((), ())),
                               preferred_element_type=jnp.float32)
        ok = mask & (gram == gram)
        w = jnp.where(ok, jnp.exp(sharpness * (gram - 1.0)), 0.0)
        return jnp.sum(w, axis=0, keepdims=True)

    totals = [jnp.zeros((1, ROWS), jnp.float32) for _ in range(GROUPS)]
    for g in range(GROUPS):
        lo = 1 if g == 0 else g * GROUP_Q
        block = pl.ds(lo, (g + 1) * GROUP_Q - lo)
        pltpu.make_async_copy(recv.at[block], recv.at[block], recv_sem.at[g]).wait()
        values = recv[g * GROUP_Q:(g + 1) * GROUP_Q].astype(jnp.float32).reshape(ROWS, D)
        scale = lax.rsqrt(jnp.sum(values * values, axis=1, keepdims=True) + epsilon)
        mine = (values * scale).astype(jnp.bfloat16)
        unit[g * ROWS:(g + 1) * ROWS] = mine
        totals[g] += weights(mine, mine, same_off)
        for h in range(g):
            other = unit[h * ROWS:(h + 1) * ROWS]
            totals[g] += weights(other, mine, same)
            totals[h] += weights(mine, other, same)

    for j in range(8):
        g, part = j // 2, j % 2
        tot[j] = totals[g][:, part * 128:(part + 1) * 128]
    ret[0] = tot[0]

    def push_back(q, _):
        back_copy(q).start()
        return 0

    lax.fori_loop(1, SHARDS, push_back, 0)
    everything = pl.ds(1, SHARDS - 1)
    pltpu.make_async_copy(ret.at[everything], ret.at[everything], back_recv).wait()

    got = ret[...].reshape(SHARDS, 128)
    q_id = lax.broadcasted_iota(jnp.int32, (SHARDS, 128), 0)
    lane = lax.broadcasted_iota(jnp.int32, (SHARDS, 128), 1)
    got = jnp.where(lane // CL == q_id % 16, got, 0.0).T
    halves[rep] = jnp.sum(got.reshape(16, CL, 128), axis=0)
    swap = pltpu.make_async_remote_copy(
        src_ref=halves.at[rep], dst_ref=halves.at[rep], send_sem=half_sem.at[0],
        recv_sem=half_sem.at[1], device_id={"rep": 1 - rep})
    swap.start()
    swap.wait()

    value = jnp.zeros((8, 128), jnp.float32)
    cluster = labels % 16
    for c in range(16):
        line = jnp.broadcast_to(halves[c // 8, c % 8:c % 8 + 1, :], (8, 128))
        value = jnp.where(cluster == c, jnp.take_along_axis(line, doc_q, axis=1), value)
    out_ref[...] = value

    pltpu.make_async_copy(send.at[everything], send.at[everything], send_sem).wait()
    pltpu.make_async_copy(ret.at[everything], ret.at[everything], back_send).wait()


def direct_totals(embeddings, labels):
    return pl.pallas_call(
        kernel,
        out_shape=jax.ShapeDtypeStruct((8, 128), jnp.float32),
        in_specs=[pl.BlockSpec(memory_space=pl.ANY), pl.BlockSpec(memory_space=pltpu.VMEM)],
        out_specs=pl.BlockSpec(memory_space=pltpu.VMEM),
        scratch_shapes=[
            pltpu.VMEM((DOCS_DEV, D), jnp.bfloat16),
            pltpu.VMEM((SHARDS, CL, D), jnp.bfloat16),
            pltpu.VMEM((SHARDS, CL, D), jnp.bfloat16),
            pltpu.VMEM((SHARDS * CL, D), jnp.bfloat16),
            pltpu.VMEM((8, 1, 128), jnp.float32),
            pltpu.VMEM((SHARDS, 1, 128), jnp.float32),
            pltpu.VMEM((2, 8, 128), jnp.float32),
            pltpu.SemaphoreType.DMA,
            pltpu.SemaphoreType.DMA,
            pltpu.SemaphoreType.DMA((GROUPS,)),
            pltpu.SemaphoreType.DMA,
            pltpu.SemaphoreType.DMA,
            pltpu.SemaphoreType.DMA((2,)),
        ],
        compiler_params=pltpu.CompilerParams(
            collective_id=0, has_side_effects=True, vmem_limit_bytes=48 * 1024 * 1024),
        name="cluster_totals",
    )(embeddings, labels.reshape(8, 128))


PLANE = 16
DEPTH = 8
SLOTS = PLANE * CL
CHIP_SLOTS = 2 * SLOTS
PACK = 160
HALF = D // 2
PAIRS = ((1, 7), (2, 6), (3, 5), (4,))
ORDER = (1, 7, 2, 6, 3, 5, 4)
FAR_Z = (4, 3, 5, 2, 6, 1, 7)
FAR_PARTS = ((10, 9, 11, 8), (6, 5, 7, 4), (14, 13, 15, 12), (2, 1, 3, 0))
FAR_PLANE = (10, 9, 11, 6, 14, 8, 2, 5, 7, 13, 15, 4, 12, 1, 3)


def prefix_rank(marks):
    i = lax.broadcasted_iota(jnp.int32, (CHIP_SLOTS, CHIP_SLOTS), 0)
    j = lax.broadcasted_iota(jnp.int32, (CHIP_SLOTS, CHIP_SLOTS), 1)
    before = jnp.where(i < j, 1.0, 0.0).astype(jnp.bfloat16)
    return jnp.dot(marks.astype(jnp.bfloat16), before, preferred_element_type=jnp.float32)


def mark_column(mark):
    return jnp.broadcast_to(mark, (128, CHIP_SLOTS)).T


def mark_absent(rows, column):
    first = jnp.where(column >= 0, rows[:, :128], jnp.nan)
    return jnp.concatenate([first, rows[:, 128:]], axis=1)


def packed_kernel(e_hbm, labels_hbm, out_ref, flag_ref, e_ref, labels_ref, zs, zr, ms, mr, ps, pr, unit, tot,
                  r1, s2, r2, load_sem, mss, mrs, zss, zrs, pss, prs, psc, prc, r1s, r1r, r1c, r2s, r2r):
    me = lax.axis_index("shard")
    rep = lax.axis_index("rep")
    y, x, z = me // 32, me // 8 % 4, me % 8
    z_dev = [y * 32 + x * 8 + (z + d) % 8 for d in range(DEPTH)]
    p_dev = [(y + p // 4) % 4 * 32 + (x + p % 4) % 4 * 8 + z for p in range(PLANE)]

    load_labels = pltpu.make_async_copy(labels_hbm, labels_ref, load_sem.at[1])
    load_labels.start()
    mine = pl.ds(pl.multiple_of(rep * HALF, HALF), HALF)
    load = pltpu.make_async_copy(e_hbm.at[:, mine], e_ref, load_sem.at[0])
    load.start()

    barrier = pltpu.get_barrier_semaphore()
    for target in [z_dev[d] for d in FAR_Z] + [p_dev[p] for p in FAR_PLANE]:
        for r in range(2):
            pl.semaphore_signal(barrier, inc=1, device_id={"shard": target, "rep": r})
    pl.semaphore_signal(barrier, inc=1, device_id={"rep": 1 - rep})
    load_labels.wait()

    labels = labels_ref[...]
    owner = labels // 16
    doc_p = (owner // 32 - y + 4) % 4 * 4 + (owner // 8 % 4 - x + 4) % 4
    doc_z = (owner % 8 - z + 8) % 8
    doc_rep = labels % 16 // 8
    doc_slot = doc_p * CL + labels % 8
    doc_chip = doc_p * 16 + labels % 16
    doc_hi = doc_chip // 128 * DEPTH + doc_z
    doc_lo = doc_chip % 128

    def onehot(count, index):
        ids = lax.broadcasted_iota(jnp.int32, (count, 128), 0)
        return jnp.concatenate(
            [jnp.where(ids == index[j:j + 1, :], 1.0, 0.0).astype(jnp.bfloat16)
             for j in range(8)], axis=1)

    marks = lax.dot_general(onehot(2 * DEPTH, doc_hi), onehot(128, doc_lo),
                            (((1,), (1,)), ((), ())), preferred_element_type=jnp.float32)
    marks = jnp.concatenate([marks[:DEPTH], marks[DEPTH:]], axis=1)
    ranks = prefix_rank(marks)
    doc_rank = jnp.zeros((8, 128), jnp.float32)
    for h in range(2):
        for d in range(DEPTH):
            line = jnp.broadcast_to(ranks[d:d + 1, h * 128:(h + 1) * 128], (8, 128))
            doc_rank = jnp.where(
                doc_hi == h * DEPTH + d, jnp.take_along_axis(line, doc_lo, axis=1), doc_rank)
    doc_rank = doc_rank.astype(jnp.int32)
    row_id = lax.broadcasted_iota(jnp.int32, (PACK, CHIP_SLOTS), 0)
    for d in range(1, DEPTH):
        ms[d] = marks[d:d + 1]

    def mark_copy(d):
        return pltpu.make_async_remote_copy(
            src_ref=ms.at[d], dst_ref=mr.at[d], send_sem=mss, recv_sem=mrs,
            device_id={"shard": z_dev[d]})

    def z_copy(d):
        return pltpu.make_async_remote_copy(
            src_ref=zs.at[d], dst_ref=zr.at[d], send_sem=zss.at[d], recv_sem=zrs.at[d],
            device_id={"shard": z_dev[d]})

    def spread(d, part, rows, column):
        low = part[-1] * 16
        rows = mark_absent(rows, column[low:low + 64])
        ps[d, part[-1]:part[-1] + 4] = rows.reshape(4, 2, CL, HALF).astype(jnp.bfloat16)
        for p in part:
            if p == 0:
                pltpu.make_async_remote_copy(
                    src_ref=ps.at[d, 0, 1 - rep], dst_ref=pr.at[d, 0, rep], send_sem=psc.at[d],
                    recv_sem=prc.at[d], device_id={"rep": 1 - rep}).start()
                pr[d, 0, rep] = ps[d, 0, rep]
                continue
            for r in range(2):
                pltpu.make_async_remote_copy(
                    src_ref=ps.at[d, p, r], dst_ref=pr.at[d, p, rep], send_sem=pss.at[d],
                    recv_sem=prs.at[d], device_id={"shard": p_dev[p], "rep": r}).start()

    def pack(group):
        select = jnp.concatenate(
            [onehot(PACK, jnp.where(doc_z == d, doc_rank, -1)) for d in group], axis=0)
        rows = jnp.dot(select, e_ref[...], preferred_element_type=jnp.float32)
        for i, d in enumerate(group):
            zs[d] = rows[i * PACK:(i + 1) * PACK].astype(jnp.bfloat16)

    load.wait()
    for group in PAIRS:
        pack(group)
    pl.semaphore_wait(barrier, 2 * (DEPTH - 1) + 2 * (PLANE - 1) + 1)
    for d in FAR_Z:
        mark_copy(d).start()
    for d in ORDER:
        z_copy(d).start()
    rows = jnp.dot(onehot(CHIP_SLOTS, jnp.where(doc_z == 0, doc_chip, -1)), e_ref[...],
                   preferred_element_type=jnp.float32)
    column = mark_column(jnp.where(marks[:1] > 0.0, 0, -1))
    for part in FAR_PARTS:
        spread(0, part, rows[part[-1] * 16:part[-1] * 16 + 64], column)

    others = pl.ds(1, PLANE - 1)
    around = pl.ds(1, DEPTH - 1)
    pltpu.make_async_copy(mr.at[around], mr.at[around], mrs).wait()
    there = jnp.concatenate([jnp.zeros((1, CHIP_SLOTS), jnp.float32)]
                            + [mr[d] for d in range(1, DEPTH)], axis=0)
    ranks = prefix_rank(there)
    full = jnp.max(ranks + there)
    ranks = jnp.where(there > 0.0, ranks, -1.0).astype(jnp.int32)

    place = lax.broadcasted_iota(jnp.int32, (CHIP_SLOTS, PACK), 1)

    def expand(d):
        column = mark_column(ranks[d:d + 1])
        wide = jnp.concatenate([column, column[:, :PACK - 128]], axis=1)
        select = jnp.where(place == wide, 1.0, 0.0).astype(jnp.bfloat16)
        pltpu.make_async_copy(zr.at[d], zr.at[d], zrs.at[d]).wait()
        rows = jnp.dot(select, zr[d], preferred_element_type=jnp.float32)
        for part in FAR_PARTS:
            spread(d, part, rows[part[-1] * 16:part[-1] * 16 + 64], column)

    i = lax.broadcasted_iota(jnp.int32, (SLOTS, SLOTS), 0)
    j = lax.broadcasted_iota(jnp.int32, (SLOTS, SLOTS), 1)
    same = i % CL == j % CL
    same_off = same & (i != j)

    def masked(a, b, mask):
        gram = lax.dot_general(a, b, (((1,), (1,)), ((), ())),
                               preferred_element_type=jnp.float32)
        ok = mask & (gram == gram)
        return jnp.where(ok, jnp.exp(sharpness * (gram - 1.0)), 0.0)

    totals = {}
    done = []

    def process(d):
        k = len(done)
        pltpu.make_async_copy(pr.at[d, others], pr.at[d, others], prs.at[d]).wait()
        pltpu.make_async_copy(pr.at[d, 0, 1 - rep], pr.at[d, 0, 1 - rep], prc.at[d]).wait()
        sides = [pr[d, :, f].astype(jnp.float32).reshape(SLOTS, HALF) for f in range(2)]
        square = jnp.sum(sides[0] * sides[0] + sides[1] * sides[1], axis=1, keepdims=True)
        scale = lax.rsqrt(square + epsilon)
        new = jnp.concatenate([(v * scale).astype(jnp.bfloat16) for v in sides], axis=1)
        unit[k * SLOTS:(k + 1) * SLOTS] = new
        both = jnp.concatenate([same] * k + [same_off], axis=0)
        grid = masked(unit[:(k + 1) * SLOTS], new, both)
        totals[d] = jnp.sum(grid, axis=0, keepdims=True)
        for n, e in enumerate(done):
            back = grid[n * SLOTS:(n + 1) * SLOTS].T
            totals[e] += jnp.sum(back, axis=0, keepdims=True)
        done.append(d)

    expand(1)
    expand(7)
    process(0)
    expand(2)
    expand(6)
    process(1)
    process(7)
    expand(3)
    expand(5)
    process(2)
    process(6)
    expand(4)
    process(3)
    process(5)
    process(4)

    table = jnp.concatenate([totals[d] for d in range(DEPTH)], axis=0)
    table = jnp.where(full > float(PACK), -1.0, table)
    for d in range(DEPTH):
        tot[d] = table[d:d + 1]

    for d in FAR_Z:
        for r in range(2):
            pltpu.make_async_remote_copy(
                src_ref=tot.at[d], dst_ref=r1.at[d, rep], send_sem=r1s, recv_sem=r1r,
                device_id={"shard": z_dev[(DEPTH - d) % DEPTH], "rep": r}).start()
    across = pltpu.make_async_remote_copy(
        src_ref=tot.at[0], dst_ref=r1.at[0, rep], send_sem=r1c.at[0], recv_sem=r1c.at[1],
        device_id={"rep": 1 - rep})
    across.start()
    r1[0, rep] = table[:1]
    pltpu.make_async_copy(r1.at[around], r1.at[around], r1r).wait()
    across.wait()

    lane = lax.broadcasted_iota(jnp.int32, (8, SLOTS), 1)
    base = lax.broadcasted_iota(jnp.int32, (8, SLOTS), 0) * CL + lane % CL
    blocks = [jnp.zeros((8, SLOTS), jnp.float32) for _ in range(2)]
    for n in range(2 * DEPTH):
        line = jnp.broadcast_to(r1[n // 2, n % 2], (8, SLOTS))
        for h in range(2):
            moved = jnp.take_along_axis(line, base + h * 64, axis=1)
            blocks[h] = jnp.where(lane // CL == n, moved, blocks[h])
    for p in (0,) + FAR_PLANE:
        s2[p] = blocks[p // 8][p % 8:p % 8 + 1]
    r2[0] = blocks[0][:1]
    for p in FAR_PLANE:
        pltpu.make_async_remote_copy(
            src_ref=s2.at[p], dst_ref=r2.at[p], send_sem=r2s, recv_sem=r2r,
            device_id={"shard": p_dev[(4 - p // 4) % 4 * 4 + (4 - p % 4) % 4]}).start()
    pltpu.make_async_copy(r2.at[others], r2.at[others], r2r).wait()

    value = jnp.zeros((8, 128), jnp.float32)
    least = jnp.zeros((1, SLOTS), jnp.float32)
    doc_lane = doc_z * 16 + labels % 16
    for p in range(PLANE):
        line = r2[p]
        least = jnp.minimum(least, line)
        found = jnp.take_along_axis(jnp.broadcast_to(line, (8, 128)), doc_lane, axis=1)
        value = jnp.where(doc_p == p, found, value)
    out_ref[...] = value
    flag_ref[0] = jnp.where(jnp.min(least) < 0.0, 1, 0).astype(jnp.int32)

    for d in ORDER:
        pltpu.make_async_copy(zs.at[d], zs.at[d], zss.at[d]).wait()
    for d in range(DEPTH):
        pltpu.make_async_copy(ps.at[d, others], ps.at[d, others], pss.at[d]).wait()
        pltpu.make_async_copy(ps.at[d, 0, 1 - rep], ps.at[d, 0, 1 - rep], psc.at[d]).wait()
    pltpu.make_async_copy(ms.at[around], ms.at[around], mss).wait()
    pltpu.make_async_copy(r1.at[around], r1.at[around], r1s).wait()
    pltpu.make_async_copy(s2.at[others], s2.at[others], r2s).wait()


def packed_totals(embeddings, labels):
    dma = pltpu.SemaphoreType.DMA
    return pl.pallas_call(
        packed_kernel,
        out_shape=(jax.ShapeDtypeStruct((8, 128), jnp.float32),
                   jax.ShapeDtypeStruct((1,), jnp.int32)),
        in_specs=[pl.BlockSpec(memory_space=pl.ANY)] * 2,
        out_specs=(pl.BlockSpec(memory_space=pltpu.VMEM), pl.BlockSpec(memory_space=pltpu.SMEM)),
        scratch_shapes=[
            pltpu.VMEM((DOCS_DEV, HALF), jnp.bfloat16),
            pltpu.VMEM((8, 128), jnp.int32),
            pltpu.VMEM((DEPTH, PACK, HALF), jnp.bfloat16),
            pltpu.VMEM((DEPTH, PACK, HALF), jnp.bfloat16),
            pltpu.VMEM((DEPTH, 1, CHIP_SLOTS), jnp.float32),
            pltpu.VMEM((DEPTH, 1, CHIP_SLOTS), jnp.float32),
            pltpu.VMEM((DEPTH, PLANE, 2, CL, HALF), jnp.bfloat16),
            pltpu.VMEM((DEPTH, PLANE, 2, CL, HALF), jnp.bfloat16),
            pltpu.VMEM((DEPTH * SLOTS, D), jnp.bfloat16),
            pltpu.VMEM((DEPTH, 1, SLOTS), jnp.float32),
            pltpu.VMEM((DEPTH, 2, 1, SLOTS), jnp.float32),
            pltpu.VMEM((PLANE, 1, SLOTS), jnp.float32),
            pltpu.VMEM((PLANE, 1, SLOTS), jnp.float32),
            dma((2,)), dma, dma, dma((DEPTH,)), dma((DEPTH,)), dma((DEPTH,)), dma((DEPTH,)),
            dma((DEPTH,)), dma((DEPTH,)), dma, dma, dma((2,)), dma, dma,
        ],
        compiler_params=pltpu.CompilerParams(
            collective_id=1, has_side_effects=True, vmem_limit_bytes=60 * 1024 * 1024),
        name="packed_totals",
    )(embeddings, labels.reshape(8, 128))


def local(embeddings, labels):
    totals, overflow = packed_totals(embeddings, labels)
    totals = lax.cond(
        overflow[0] > 0, lambda: direct_totals(embeddings, labels), lambda: totals)
    return jnp.log1p(totals.reshape(DOCS_DEV))


def solution(mesh):
    return jax.shard_map(
        local,
        mesh=mesh,
        in_specs=(P("shard", None), P("shard")),
        out_specs=P("shard"),
        check_vma=False,
    )
```

```python
import functools
import jax
import jax.numpy as jnp
from jax import lax
from jax.experimental import pallas as pl
from jax.experimental.pallas import tpu as pltpu
from jax.sharding import PartitionSpec as P

SHARDS = 128
DOCS_DEV = 1024
D = 1024
CL = 8
GROUPS = 4
GROUP_Q = SHARDS // GROUPS
ROWS = GROUP_Q * CL

sharpness = 4.0
epsilon = 1e-06


def offset_of(q):
    k = q % 8
    dz = jnp.where(k % 2 == 1, (k + 1) // 2, (8 - k // 2) % 8)
    return (q // 32) % 4, (q // 8) % 4, dz


def q_of(dy, dx, dz):
    k = jnp.where(dz == 0, 0, jnp.where(dz <= 4, 2 * dz - 1, 2 * (8 - dz)))
    return dy * 32 + dx * 8 + k


def shift(s, q, sign):
    dy, dx, dz = offset_of(q)
    y = (s // 32 + 4 + sign * dy) % 4
    x = (s // 8 % 4 + 4 + sign * dx) % 4
    z = (s % 8 + 8 + sign * dz) % 8
    return y * 32 + x * 8 + z


def kernel(e_hbm, labels_ref, out_ref, e_ref, send, recv, unit, tot, ret, halves,
           load_sem, send_sem, recv_sem, back_send, back_recv, half_sem):
    me = lax.axis_index("shard")
    rep = lax.axis_index("rep")
    load = pltpu.make_async_copy(e_hbm, e_ref, load_sem)
    load.start()

    barrier = pltpu.get_barrier_semaphore()

    def greet(q, _):
        pl.semaphore_signal(barrier, inc=1, device_id={"shard": shift(me, q, -1)})
        return 0

    lax.fori_loop(1, SHARDS, greet, 0)
    pl.semaphore_signal(barrier, inc=1, device_id={"rep": 1 - rep})
    load.wait()

    labels = labels_ref[...]
    owner = labels // 16
    dy = (owner // 32 - me // 32 + 4) % 4
    dx = (owner // 8 % 4 - me // 8 % 4 + 4) % 4
    dz = (owner % 8 - me % 8 + 8) % 8
    doc_q = q_of(dy, dx, dz)
    doc_slot = jnp.where(labels % 16 // 8 == rep, doc_q * 8 + labels % 8, -1)

    def row_copy(q):
        return pltpu.make_async_remote_copy(
            src_ref=send.at[q], dst_ref=recv.at[q], send_sem=send_sem,
            recv_sem=recv_sem.at[q // GROUP_Q],
            device_id={"shard": shift(me, q, 1)})

    def back_copy(q):
        return pltpu.make_async_remote_copy(
            src_ref=tot.at[q // 16], dst_ref=ret.at[q], send_sem=back_send,
            recv_sem=back_recv, device_id={"shard": shift(me, q, -1)})

    def fill(g):
        ids = lax.broadcasted_iota(jnp.int32, (ROWS, 128), 0) + g * ROWS
        hits = [ids == doc_slot[j:j + 1, :] for j in range(8)]
        onehot = jnp.concatenate(
            [jnp.where(h, 1.0, 0.0).astype(jnp.bfloat16) for h in hits], axis=1)
        any_hit = functools.reduce(
            jnp.add, [jnp.where(h, 1.0, 0.0) for h in hits])
        present = jnp.sum(any_hit, axis=1, keepdims=True) > 0.0
        rows = jnp.dot(onehot, e_ref[...], preferred_element_type=jnp.float32)
        rows = jnp.where(present, rows, jnp.nan)
        rows = rows.reshape(GROUP_Q, CL, D).astype(jnp.bfloat16)
        send[g * GROUP_Q:(g + 1) * GROUP_Q] = rows
        if g == 0:
            recv[0] = rows[0]

    for g in range(GROUPS):
        fill(g)
        if g == 0:
            pl.semaphore_wait(barrier, SHARDS)

        def push(q, _):
            row_copy(q).start()
            return 0

        lax.fori_loop(1 if g == 0 else g * GROUP_Q, (g + 1) * GROUP_Q, push, 0)

    row_id = lax.broadcasted_iota(jnp.int32, (ROWS, ROWS), 0)
    col_id = lax.broadcasted_iota(jnp.int32, (ROWS, ROWS), 1)
    same = row_id % CL == col_id % CL
    same_off = same & (row_id != col_id)

    def weights(a, b, mask):
        gram = lax.dot_general(a, b, (((1,), (1,)), ((), ())),
                               preferred_element_type=jnp.float32)
        ok = mask & (gram == gram)
        w = jnp.where(ok, jnp.exp(sharpness * (gram - 1.0)), 0.0)
        return jnp.sum(w, axis=0, keepdims=True)

    totals = [jnp.zeros((1, ROWS), jnp.float32) for _ in range(GROUPS)]
    for g in range(GROUPS):
        lo = 1 if g == 0 else g * GROUP_Q
        block = pl.ds(lo, (g + 1) * GROUP_Q - lo)
        pltpu.make_async_copy(recv.at[block], recv.at[block], recv_sem.at[g]).wait()
        values = recv[g * GROUP_Q:(g + 1) * GROUP_Q].astype(jnp.float32).reshape(ROWS, D)
        scale = lax.rsqrt(jnp.sum(values * values, axis=1, keepdims=True) + epsilon)
        mine = (values * scale).astype(jnp.bfloat16)
        unit[g * ROWS:(g + 1) * ROWS] = mine
        totals[g] += weights(mine, mine, same_off)
        for h in range(g):
            other = unit[h * ROWS:(h + 1) * ROWS]
            totals[g] += weights(other, mine, same)
            totals[h] += weights(mine, other, same)

    for j in range(8):
        g, part = j // 2, j % 2
        tot[j] = totals[g][:, part * 128:(part + 1) * 128]
    ret[0] = tot[0]

    def push_back(q, _):
        back_copy(q).start()
        return 0

    lax.fori_loop(1, SHARDS, push_back, 0)
    everything = pl.ds(1, SHARDS - 1)
    pltpu.make_async_copy(ret.at[everything], ret.at[everything], back_recv).wait()

    got = ret[...].reshape(SHARDS, 128)
    q_id = lax.broadcasted_iota(jnp.int32, (SHARDS, 128), 0)
    lane = lax.broadcasted_iota(jnp.int32, (SHARDS, 128), 1)
    got = jnp.where(lane // CL == q_id % 16, got, 0.0).T
    halves[rep] = jnp.sum(got.reshape(16, CL, 128), axis=0)
    swap = pltpu.make_async_remote_copy(
        src_ref=halves.at[rep], dst_ref=halves.at[rep], send_sem=half_sem.at[0],
        recv_sem=half_sem.at[1], device_id={"rep": 1 - rep})
    swap.start()
    swap.wait()

    value = jnp.zeros((8, 128), jnp.float32)
    cluster = labels % 16
    for c in range(16):
        line = jnp.broadcast_to(halves[c // 8, c % 8:c % 8 + 1, :], (8, 128))
        value = jnp.where(cluster == c, jnp.take_along_axis(line, doc_q, axis=1), value)
    out_ref[...] = value

    pltpu.make_async_copy(send.at[everything], send.at[everything], send_sem).wait()
    pltpu.make_async_copy(ret.at[everything], ret.at[everything], back_send).wait()


def direct_totals(embeddings, labels):
    return pl.pallas_call(
        kernel,
        out_shape=jax.ShapeDtypeStruct((8, 128), jnp.float32),
        in_specs=[pl.BlockSpec(memory_space=pl.ANY), pl.BlockSpec(memory_space=pltpu.VMEM)],
        out_specs=pl.BlockSpec(memory_space=pltpu.VMEM),
        scratch_shapes=[
            pltpu.VMEM((DOCS_DEV, D), jnp.bfloat16),
            pltpu.VMEM((SHARDS, CL, D), jnp.bfloat16),
            pltpu.VMEM((SHARDS, CL, D), jnp.bfloat16),
            pltpu.VMEM((SHARDS * CL, D), jnp.bfloat16),
            pltpu.VMEM((8, 1, 128), jnp.float32),
            pltpu.VMEM((SHARDS, 1, 128), jnp.float32),
            pltpu.VMEM((2, 8, 128), jnp.float32),
            pltpu.SemaphoreType.DMA,
            pltpu.SemaphoreType.DMA,
            pltpu.SemaphoreType.DMA((GROUPS,)),
            pltpu.SemaphoreType.DMA,
            pltpu.SemaphoreType.DMA,
            pltpu.SemaphoreType.DMA((2,)),
        ],
        compiler_params=pltpu.CompilerParams(
            collective_id=0, has_side_effects=True, vmem_limit_bytes=48 * 1024 * 1024),
        name="cluster_totals",
    )(embeddings, labels.reshape(8, 128))


PLANE = 16
DEPTH = 8
SLOTS = PLANE * CL
CHIP_SLOTS = 2 * SLOTS
PACK = 160
HALF = D // 2
PAIRS = ((1, 7), (2, 6), (3, 5), (4,))
ORDER = (1, 7, 2, 6, 3, 5, 4)
FAR_Z = (4, 3, 5, 2, 6, 1, 7)
FAR_PARTS = ((10, 9, 11, 8), (6, 5, 7, 4), (14, 13, 15, 12), (2, 1, 3, 0))
FAR_PLANE = (10, 9, 11, 6, 14, 8, 2, 5, 7, 13, 15, 4, 12, 1, 3)


def prefix_rank(marks):
    i = lax.broadcasted_iota(jnp.int32, (CHIP_SLOTS, CHIP_SLOTS), 0)
    j = lax.broadcasted_iota(jnp.int32, (CHIP_SLOTS, CHIP_SLOTS), 1)
    before = jnp.where(i < j, 1.0, 0.0).astype(jnp.bfloat16)
    return jnp.dot(marks.astype(jnp.bfloat16), before, preferred_element_type=jnp.float32)


def mark_column(mark):
    return jnp.broadcast_to(mark, (128, CHIP_SLOTS)).T


def mark_absent(rows, column):
    first = jnp.where(column >= 0, rows[:, :128], jnp.nan)
    return jnp.concatenate([first, rows[:, 128:]], axis=1)


def packed_kernel(e_hbm, labels_hbm, out_ref, flag_ref, e_ref, labels_ref, zs, zr, ms, mr, ps, pr, unit, tot,
                  r1, s2, r2, load_sem, mss, mrs, zss, zrs, pss, prs, psc, prc, r1s, r1r, r1c, r2s, r2r):
    me = lax.axis_index("shard")
    rep = lax.axis_index("rep")
    y, x, z = me // 32, me // 8 % 4, me % 8
    z_dev = [y * 32 + x * 8 + (z + d) % 8 for d in range(DEPTH)]
    p_dev = [(y + p // 4) % 4 * 32 + (x + p % 4) % 4 * 8 + z for p in range(PLANE)]

    load_labels = pltpu.make_async_copy(labels_hbm, labels_ref, load_sem.at[1])
    load_labels.start()
    mine = pl.ds(pl.multiple_of(rep * HALF, HALF), HALF)
    load = pltpu.make_async_copy(e_hbm.at[:, mine], e_ref, load_sem.at[0])
    load.start()

    barrier = pltpu.get_barrier_semaphore()
    for target in [z_dev[d] for d in FAR_Z] + [p_dev[p] for p in FAR_PLANE]:
        for r in range(2):
            pl.semaphore_signal(barrier, inc=1, device_id={"shard": target, "rep": r})
    pl.semaphore_signal(barrier, inc=1, device_id={"rep": 1 - rep})
    load_labels.wait()

    labels = labels_ref[...]
    owner = labels // 16
    doc_p = (owner // 32 - y + 4) % 4 * 4 + (owner // 8 % 4 - x + 4) % 4
    doc_z = (owner % 8 - z + 8) % 8
    doc_rep = labels % 16 // 8
    doc_slot = doc_p * CL + labels % 8
    doc_chip = doc_p * 16 + labels % 16
    doc_hi = doc_chip // 128 * DEPTH + doc_z
    doc_lo = doc_chip % 128

    def onehot(count, index):
        ids = lax.broadcasted_iota(jnp.int32, (count, 128), 0)
        return jnp.concatenate(
            [jnp.where(ids == index[j:j + 1, :], 1.0, 0.0).astype(jnp.bfloat16)
             for j in range(8)], axis=1)

    marks = lax.dot_general(onehot(2 * DEPTH, doc_hi), onehot(128, doc_lo),
                            (((1,), (1,)), ((), ())), preferred_element_type=jnp.float32)
    marks = jnp.concatenate([marks[:DEPTH], marks[DEPTH:]], axis=1)
    ranks = prefix_rank(marks)
    doc_rank = jnp.zeros((8, 128), jnp.float32)
    for h in range(2):
        for d in range(DEPTH):
            line = jnp.broadcast_to(ranks[d:d + 1, h * 128:(h + 1) * 128], (8, 128))
            doc_rank = jnp.where(
                doc_hi == h * DEPTH + d, jnp.take_along_axis(line, doc_lo, axis=1), doc_rank)
    doc_rank = doc_rank.astype(jnp.int32)
    row_id = lax.broadcasted_iota(jnp.int32, (PACK, CHIP_SLOTS), 0)
    for d in range(1, DEPTH):
        ms[d] = marks[d:d + 1]

    def mark_copy(d):
        return pltpu.make_async_remote_copy(
            src_ref=ms.at[d], dst_ref=mr.at[d], send_sem=mss, recv_sem=mrs,
            device_id={"shard": z_dev[d]})

    def z_copy(d):
        return pltpu.make_async_remote_copy(
            src_ref=zs.at[d], dst_ref=zr.at[d], send_sem=zss.at[d], recv_sem=zrs.at[d],
            device_id={"shard": z_dev[d]})

    def spread(d, part, rows, column):
        low = part[-1] * 16
        rows = mark_absent(rows, column[low:low + 64])
        ps[d, part[-1]:part[-1] + 4] = rows.reshape(4, 2, CL, HALF).astype(jnp.bfloat16)
        for p in part:
            if p == 0:
                pltpu.make_async_remote_copy(
                    src_ref=ps.at[d, 0, 1 - rep], dst_ref=pr.at[d, 0, rep], send_sem=psc.at[d],
                    recv_sem=prc.at[d], device_id={"rep": 1 - rep}).start()
                pr[d, 0, rep] = ps[d, 0, rep]
                continue
            for r in range(2):
                pltpu.make_async_remote_copy(
                    src_ref=ps.at[d, p, r], dst_ref=pr.at[d, p, rep], send_sem=pss.at[d],
                    recv_sem=prs.at[d], device_id={"shard": p_dev[p], "rep": r}).start()

    def pack(group):
        select = jnp.concatenate(
            [onehot(PACK, jnp.where(doc_z == d, doc_rank, -1)) for d in group], axis=0)
        rows = jnp.dot(select, e_ref[...], preferred_element_type=jnp.float32)
        for i, d in enumerate(group):
            zs[d] = rows[i * PACK:(i + 1) * PACK].astype(jnp.bfloat16)

    load.wait()
    for group in PAIRS:
        pack(group)
    pl.semaphore_wait(barrier, 2 * (DEPTH - 1) + 2 * (PLANE - 1) + 1)
    for d in FAR_Z:
        mark_copy(d).start()
    for d in ORDER:
        z_copy(d).start()
    rows = jnp.dot(onehot(CHIP_SLOTS, jnp.where(doc_z == 0, doc_chip, -1)), e_ref[...],
                   preferred_element_type=jnp.float32)
    column = mark_column(jnp.where(marks[:1] > 0.0, 0, -1))
    for part in FAR_PARTS:
        spread(0, part, rows[part[-1] * 16:part[-1] * 16 + 64], column)

    others = pl.ds(1, PLANE - 1)
    around = pl.ds(1, DEPTH - 1)
    pltpu.make_async_copy(mr.at[around], mr.at[around], mrs).wait()
    there = jnp.concatenate([jnp.zeros((1, CHIP_SLOTS), jnp.float32)]
                            + [mr[d] for d in range(1, DEPTH)], axis=0)
    ranks = prefix_rank(there)
    full = jnp.max(ranks + there)
    ranks = jnp.where(there > 0.0, ranks, -1.0).astype(jnp.int32)

    place = lax.broadcasted_iota(jnp.int32, (CHIP_SLOTS, PACK), 1)

    def expand(d):
        column = mark_column(ranks[d:d + 1])
        wide = jnp.concatenate([column, column[:, :PACK - 128]], axis=1)
        select = jnp.where(place == wide, 1.0, 0.0).astype(jnp.bfloat16)
        pltpu.make_async_copy(zr.at[d], zr.at[d], zrs.at[d]).wait()
        rows = jnp.dot(select, zr[d], preferred_element_type=jnp.float32)
        for part in FAR_PARTS:
            spread(d, part, rows[part[-1] * 16:part[-1] * 16 + 64], column)

    i = lax.broadcasted_iota(jnp.int32, (SLOTS, SLOTS), 0)
    j = lax.broadcasted_iota(jnp.int32, (SLOTS, SLOTS), 1)
    same = i % CL == j % CL
    same_off = same & (i != j)

    def masked(a, b, mask):
        gram = lax.dot_general(a, b, (((1,), (1,)), ((), ())),
                               preferred_element_type=jnp.float32)
        ok = mask & (gram == gram)
        return jnp.where(ok, jnp.exp(sharpness * (gram - 1.0)), 0.0)

    totals = {}
    done = []

    def process(d):
        k = len(done)
        pltpu.make_async_copy(pr.at[d, others], pr.at[d, others], prs.at[d]).wait()
        pltpu.make_async_copy(pr.at[d, 0, 1 - rep], pr.at[d, 0, 1 - rep], prc.at[d]).wait()
        sides = [pr[d, :, f].astype(jnp.float32).reshape(SLOTS, HALF) for f in range(2)]
        square = jnp.sum(sides[0] * sides[0] + sides[1] * sides[1], axis=1, keepdims=True)
        scale = lax.rsqrt(square + epsilon)
        new = jnp.concatenate([(v * scale).astype(jnp.bfloat16) for v in sides], axis=1)
        unit[k * SLOTS:(k + 1) * SLOTS] = new
        both = jnp.concatenate([same] * k + [same_off], axis=0)
        grid = masked(unit[:(k + 1) * SLOTS], new, both)
        totals[d] = jnp.sum(grid, axis=0, keepdims=True)
        for n, e in enumerate(done):
            back = grid[n * SLOTS:(n + 1) * SLOTS].T
            totals[e] += jnp.sum(back, axis=0, keepdims=True)
        done.append(d)

    expand(1)
    expand(7)
    process(0)
    expand(2)
    expand(6)
    process(1)
    process(7)
    expand(3)
    expand(5)
    process(2)
    process(6)
    expand(4)
    process(3)
    process(5)
    process(4)

    table = jnp.concatenate([totals[d] for d in range(DEPTH)], axis=0)
    table = jnp.where(full > float(PACK), -1.0, table)
    for d in range(DEPTH):
        tot[d] = table[d:d + 1]

    for d in FAR_Z:
        for r in range(2):
            pltpu.make_async_remote_copy(
                src_ref=tot.at[d], dst_ref=r1.at[d, rep], send_sem=r1s, recv_sem=r1r,
                device_id={"shard": z_dev[(DEPTH - d) % DEPTH], "rep": r}).start()
    across = pltpu.make_async_remote_copy(
        src_ref=tot.at[0], dst_ref=r1.at[0, rep], send_sem=r1c.at[0], recv_sem=r1c.at[1],
        device_id={"rep": 1 - rep})
    across.start()
    r1[0, rep] = table[:1]
    pltpu.make_async_copy(r1.at[around], r1.at[around], r1r).wait()
    across.wait()

    lane = lax.broadcasted_iota(jnp.int32, (8, SLOTS), 1)
    base = lax.broadcasted_iota(jnp.int32, (8, SLOTS), 0) * CL + lane % CL
    for h, far in ((1, (10, 9, 11, 8, 14, 13, 15, 12)), (0, (6, 2, 5, 7, 4, 1, 3, 0))):
        block = jnp.zeros((8, SLOTS), jnp.float32)
        for n in range(2 * DEPTH):
            line = jnp.broadcast_to(r1[n // 2, n % 2], (8, SLOTS))
            moved = jnp.take_along_axis(line, base + h * 64, axis=1)
            block = jnp.where(lane // CL == n, moved, block)
        for p in far:
            s2[p] = block[p % 8:p % 8 + 1]
        for p in far:
            if p == 0:
                r2[0] = block[:1]
                continue
            pltpu.make_async_remote_copy(
                src_ref=s2.at[p], dst_ref=r2.at[p], send_sem=r2s, recv_sem=r2r,
                device_id={"shard": p_dev[(4 - p // 4) % 4 * 4 + (4 - p % 4) % 4]}).start()
    for d in ORDER:
        pltpu.make_async_copy(zs.at[d], zs.at[d], zss.at[d]).wait()
    for d in range(DEPTH):
        pltpu.make_async_copy(ps.at[d, others], ps.at[d, others], pss.at[d]).wait()
        pltpu.make_async_copy(ps.at[d, 0, 1 - rep], ps.at[d, 0, 1 - rep], psc.at[d]).wait()
    pltpu.make_async_copy(ms.at[around], ms.at[around], mss).wait()
    pltpu.make_async_copy(r1.at[around], r1.at[around], r1s).wait()
    pltpu.make_async_copy(r2.at[others], r2.at[others], r2r).wait()

    value = jnp.zeros((8, 128), jnp.float32)
    least = jnp.zeros((1, SLOTS), jnp.float32)
    doc_lane = doc_z * 16 + labels % 16
    for p in range(PLANE):
        line = r2[p]
        least = jnp.minimum(least, line)
        found = jnp.take_along_axis(jnp.broadcast_to(line, (8, 128)), doc_lane, axis=1)
        value = jnp.where(doc_p == p, found, value)
    out_ref[...] = value
    flag_ref[0] = jnp.where(jnp.min(least) < 0.0, 1, 0).astype(jnp.int32)

    pltpu.make_async_copy(s2.at[others], s2.at[others], r2s).wait()


def packed_totals(embeddings, labels):
    dma = pltpu.SemaphoreType.DMA
    return pl.pallas_call(
        packed_kernel,
        out_shape=(jax.ShapeDtypeStruct((8, 128), jnp.float32),
                   jax.ShapeDtypeStruct((1,), jnp.int32)),
        in_specs=[pl.BlockSpec(memory_space=pl.ANY)] * 2,
        out_specs=(pl.BlockSpec(memory_space=pltpu.VMEM), pl.BlockSpec(memory_space=pltpu.SMEM)),
        scratch_shapes=[
            pltpu.VMEM((DOCS_DEV, HALF), jnp.bfloat16),
            pltpu.VMEM((8, 128), jnp.int32),
            pltpu.VMEM((DEPTH, PACK, HALF), jnp.bfloat16),
            pltpu.VMEM((DEPTH, PACK, HALF), jnp.bfloat16),
            pltpu.VMEM((DEPTH, 1, CHIP_SLOTS), jnp.float32),
            pltpu.VMEM((DEPTH, 1, CHIP_SLOTS), jnp.float32),
            pltpu.VMEM((DEPTH, PLANE, 2, CL, HALF), jnp.bfloat16),
            pltpu.VMEM((DEPTH, PLANE, 2, CL, HALF), jnp.bfloat16),
            pltpu.VMEM((DEPTH * SLOTS, D), jnp.bfloat16),
            pltpu.VMEM((DEPTH, 1, SLOTS), jnp.float32),
            pltpu.VMEM((DEPTH, 2, 1, SLOTS), jnp.float32),
            pltpu.VMEM((PLANE, 1, SLOTS), jnp.float32),
            pltpu.VMEM((PLANE, 1, SLOTS), jnp.float32),
            dma((2,)), dma, dma, dma((DEPTH,)), dma((DEPTH,)), dma((DEPTH,)), dma((DEPTH,)),
            dma((DEPTH,)), dma((DEPTH,)), dma, dma, dma((2,)), dma, dma,
        ],
        compiler_params=pltpu.CompilerParams(
            collective_id=1, has_side_effects=True, vmem_limit_bytes=60 * 1024 * 1024),
        name="packed_totals",
    )(embeddings, labels.reshape(8, 128))


def local(embeddings, labels):
    totals, overflow = packed_totals(embeddings, labels)
    totals = lax.cond(
        overflow[0] > 0, lambda: direct_totals(embeddings, labels), lambda: totals)
    return jnp.log1p(totals.reshape(DOCS_DEV))


def solution(mesh):
    return jax.shard_map(
        local,
        mesh=mesh,
        in_specs=(P("shard", None), P("shard")),
        out_specs=P("shard"),
        check_vma=False,
    )
```

```python
import functools
import jax
import jax.numpy as jnp
from jax import lax
from jax.experimental import pallas as pl
from jax.experimental.pallas import tpu as pltpu
from jax.sharding import PartitionSpec as P

SHARDS = 128
DOCS_DEV = 1024
D = 1024
CL = 8
GROUPS = 4
GROUP_Q = SHARDS // GROUPS
ROWS = GROUP_Q * CL

sharpness = 4.0
epsilon = 1e-06


def offset_of(q):
    k = q % 8
    dz = jnp.where(k % 2 == 1, (k + 1) // 2, (8 - k // 2) % 8)
    return (q // 32) % 4, (q // 8) % 4, dz


def q_of(dy, dx, dz):
    k = jnp.where(dz == 0, 0, jnp.where(dz <= 4, 2 * dz - 1, 2 * (8 - dz)))
    return dy * 32 + dx * 8 + k


def shift(s, q, sign):
    dy, dx, dz = offset_of(q)
    y = (s // 32 + 4 + sign * dy) % 4
    x = (s // 8 % 4 + 4 + sign * dx) % 4
    z = (s % 8 + 8 + sign * dz) % 8
    return y * 32 + x * 8 + z


def kernel(e_hbm, labels_ref, out_ref, e_ref, send, recv, unit, tot, ret, halves,
           load_sem, send_sem, recv_sem, back_send, back_recv, half_sem):
    me = lax.axis_index("shard")
    rep = lax.axis_index("rep")
    load = pltpu.make_async_copy(e_hbm, e_ref, load_sem)
    load.start()

    barrier = pltpu.get_barrier_semaphore()

    def greet(q, _):
        pl.semaphore_signal(barrier, inc=1, device_id={"shard": shift(me, q, -1)})
        return 0

    lax.fori_loop(1, SHARDS, greet, 0)
    pl.semaphore_signal(barrier, inc=1, device_id={"rep": 1 - rep})
    load.wait()

    labels = labels_ref[...]
    owner = labels // 16
    dy = (owner // 32 - me // 32 + 4) % 4
    dx = (owner // 8 % 4 - me // 8 % 4 + 4) % 4
    dz = (owner % 8 - me % 8 + 8) % 8
    doc_q = q_of(dy, dx, dz)
    doc_slot = jnp.where(labels % 16 // 8 == rep, doc_q * 8 + labels % 8, -1)

    def row_copy(q):
        return pltpu.make_async_remote_copy(
            src_ref=send.at[q], dst_ref=recv.at[q], send_sem=send_sem,
            recv_sem=recv_sem.at[q // GROUP_Q],
            device_id={"shard": shift(me, q, 1)})

    def back_copy(q):
        return pltpu.make_async_remote_copy(
            src_ref=tot.at[q // 16], dst_ref=ret.at[q], send_sem=back_send,
            recv_sem=back_recv, device_id={"shard": shift(me, q, -1)})

    def fill(g):
        ids = lax.broadcasted_iota(jnp.int32, (ROWS, 128), 0) + g * ROWS
        hits = [ids == doc_slot[j:j + 1, :] for j in range(8)]
        onehot = jnp.concatenate(
            [jnp.where(h, 1.0, 0.0).astype(jnp.bfloat16) for h in hits], axis=1)
        any_hit = functools.reduce(
            jnp.add, [jnp.where(h, 1.0, 0.0) for h in hits])
        present = jnp.sum(any_hit, axis=1, keepdims=True) > 0.0
        rows = jnp.dot(onehot, e_ref[...], preferred_element_type=jnp.float32)
        rows = jnp.where(present, rows, jnp.nan)
        rows = rows.reshape(GROUP_Q, CL, D).astype(jnp.bfloat16)
        send[g * GROUP_Q:(g + 1) * GROUP_Q] = rows
        if g == 0:
            recv[0] = rows[0]

    for g in range(GROUPS):
        fill(g)
        if g == 0:
            pl.semaphore_wait(barrier, SHARDS)

        def push(q, _):
            row_copy(q).start()
            return 0

        lax.fori_loop(1 if g == 0 else g * GROUP_Q, (g + 1) * GROUP_Q, push, 0)

    row_id = lax.broadcasted_iota(jnp.int32, (ROWS, ROWS), 0)
    col_id = lax.broadcasted_iota(jnp.int32, (ROWS, ROWS), 1)
    same = row_id % CL == col_id % CL
    same_off = same & (row_id != col_id)

    def weights(a, b, mask):
        gram = lax.dot_general(a, b, (((1,), (1,)), ((), ())),
                               preferred_element_type=jnp.float32)
        ok = mask & (gram == gram)
        w = jnp.where(ok, jnp.exp(sharpness * (gram - 1.0)), 0.0)
        return jnp.sum(w, axis=0, keepdims=True)

    totals = [jnp.zeros((1, ROWS), jnp.float32) for _ in range(GROUPS)]
    for g in range(GROUPS):
        lo = 1 if g == 0 else g * GROUP_Q
        block = pl.ds(lo, (g + 1) * GROUP_Q - lo)
        pltpu.make_async_copy(recv.at[block], recv.at[block], recv_sem.at[g]).wait()
        values = recv[g * GROUP_Q:(g + 1) * GROUP_Q].astype(jnp.float32).reshape(ROWS, D)
        scale = lax.rsqrt(jnp.sum(values * values, axis=1, keepdims=True) + epsilon)
        mine = (values * scale).astype(jnp.bfloat16)
        unit[g * ROWS:(g + 1) * ROWS] = mine
        totals[g] += weights(mine, mine, same_off)
        for h in range(g):
            other = unit[h * ROWS:(h + 1) * ROWS]
            totals[g] += weights(other, mine, same)
            totals[h] += weights(mine, other, same)

    for j in range(8):
        g, part = j // 2, j % 2
        tot[j] = totals[g][:, part * 128:(part + 1) * 128]
    ret[0] = tot[0]

    def push_back(q, _):
        back_copy(q).start()
        return 0

    lax.fori_loop(1, SHARDS, push_back, 0)
    everything = pl.ds(1, SHARDS - 1)
    pltpu.make_async_copy(ret.at[everything], ret.at[everything], back_recv).wait()

    got = ret[...].reshape(SHARDS, 128)
    q_id = lax.broadcasted_iota(jnp.int32, (SHARDS, 128), 0)
    lane = lax.broadcasted_iota(jnp.int32, (SHARDS, 128), 1)
    got = jnp.where(lane // CL == q_id % 16, got, 0.0).T
    halves[rep] = jnp.sum(got.reshape(16, CL, 128), axis=0)
    swap = pltpu.make_async_remote_copy(
        src_ref=halves.at[rep], dst_ref=halves.at[rep], send_sem=half_sem.at[0],
        recv_sem=half_sem.at[1], device_id={"rep": 1 - rep})
    swap.start()
    swap.wait()

    value = jnp.zeros((8, 128), jnp.float32)
    cluster = labels % 16
    for c in range(16):
        line = jnp.broadcast_to(halves[c // 8, c % 8:c % 8 + 1, :], (8, 128))
        value = jnp.where(cluster == c, jnp.take_along_axis(line, doc_q, axis=1), value)
    out_ref[...] = value

    pltpu.make_async_copy(send.at[everything], send.at[everything], send_sem).wait()
    pltpu.make_async_copy(ret.at[everything], ret.at[everything], back_send).wait()


def direct_totals(embeddings, labels):
    return pl.pallas_call(
        kernel,
        out_shape=jax.ShapeDtypeStruct((8, 128), jnp.float32),
        in_specs=[pl.BlockSpec(memory_space=pl.ANY), pl.BlockSpec(memory_space=pltpu.VMEM)],
        out_specs=pl.BlockSpec(memory_space=pltpu.VMEM),
        scratch_shapes=[
            pltpu.VMEM((DOCS_DEV, D), jnp.bfloat16),
            pltpu.VMEM((SHARDS, CL, D), jnp.bfloat16),
            pltpu.VMEM((SHARDS, CL, D), jnp.bfloat16),
            pltpu.VMEM((SHARDS * CL, D), jnp.bfloat16),
            pltpu.VMEM((8, 1, 128), jnp.float32),
            pltpu.VMEM((SHARDS, 1, 128), jnp.float32),
            pltpu.VMEM((2, 8, 128), jnp.float32),
            pltpu.SemaphoreType.DMA,
            pltpu.SemaphoreType.DMA,
            pltpu.SemaphoreType.DMA((GROUPS,)),
            pltpu.SemaphoreType.DMA,
            pltpu.SemaphoreType.DMA,
            pltpu.SemaphoreType.DMA((2,)),
        ],
        compiler_params=pltpu.CompilerParams(
            collective_id=0, has_side_effects=True, vmem_limit_bytes=48 * 1024 * 1024),
        name="cluster_totals",
    )(embeddings, labels.reshape(8, 128))


PLANE = 16
DEPTH = 8
SLOTS = PLANE * CL
CHIP_SLOTS = 2 * SLOTS
PACK = 160
HALF = D // 2
PAIRS = ((1, 7), (2, 6), (3, 5), (4,))
ORDER = (1, 7, 2, 6, 3, 5, 4)
FAR_Z = (4, 3, 5, 2, 6, 1, 7)
FAR_PARTS = ((10, 9, 11, 8), (6, 5, 7, 4), (14, 13, 15, 12), (2, 1, 3, 0))
FAR_PLANE = (10, 9, 11, 6, 14, 8, 2, 5, 7, 13, 15, 4, 12, 1, 3)


def prefix_rank(marks):
    i = lax.broadcasted_iota(jnp.int32, (CHIP_SLOTS, CHIP_SLOTS), 0)
    j = lax.broadcasted_iota(jnp.int32, (CHIP_SLOTS, CHIP_SLOTS), 1)
    before = jnp.where(i < j, 1.0, 0.0).astype(jnp.bfloat16)
    return jnp.dot(marks.astype(jnp.bfloat16), before, preferred_element_type=jnp.float32)


def mark_column(mark):
    return jnp.broadcast_to(mark, (128, CHIP_SLOTS)).T


def mark_absent(rows, column):
    first = jnp.where(column >= 0, rows[:, :128], jnp.nan)
    return jnp.concatenate([first, rows[:, 128:]], axis=1)


def packed_kernel(e_hbm, labels_hbm, out_ref, flag_ref, e_ref, labels_ref, zs, zr, ms, mr, ps, pr, unit, tot,
                  r1, s2, r2, load_sem, mss, mrs, zss, zrs, pss, prs, psc, prc, r1s, r1r, r1c, r2s, r2r):
    me = lax.axis_index("shard")
    rep = lax.axis_index("rep")
    y, x, z = me // 32, me // 8 % 4, me % 8
    z_dev = [y * 32 + x * 8 + (z + d) % 8 for d in range(DEPTH)]
    p_dev = [(y + p // 4) % 4 * 32 + (x + p % 4) % 4 * 8 + z for p in range(PLANE)]

    barrier = pltpu.get_barrier_semaphore()
    for target in [z_dev[d] for d in FAR_Z] + [p_dev[p] for p in FAR_PLANE]:
        for r in range(2):
            pl.semaphore_signal(barrier, inc=1, device_id={"shard": target, "rep": r})
    pl.semaphore_signal(barrier, inc=1, device_id={"rep": 1 - rep})
    load_labels = pltpu.make_async_copy(labels_hbm, labels_ref, load_sem.at[1])
    load_labels.start()
    mine = pl.ds(pl.multiple_of(rep * HALF, HALF), HALF)
    load = pltpu.make_async_copy(e_hbm.at[:, mine], e_ref, load_sem.at[0])
    load.start()
    load_labels.wait()

    labels = labels_ref[...]
    owner = labels // 16
    doc_p = (owner // 32 - y + 4) % 4 * 4 + (owner // 8 % 4 - x + 4) % 4
    doc_z = (owner % 8 - z + 8) % 8
    doc_rep = labels % 16 // 8
    doc_slot = doc_p * CL + labels % 8
    doc_chip = doc_p * 16 + labels % 16
    doc_hi = doc_chip // 128 * DEPTH + doc_z
    doc_lo = doc_chip % 128

    def onehot(count, index):
        ids = lax.broadcasted_iota(jnp.int32, (count, 128), 0)
        return jnp.concatenate(
            [jnp.where(ids == index[j:j + 1, :], 1.0, 0.0).astype(jnp.bfloat16)
             for j in range(8)], axis=1)

    marks = lax.dot_general(onehot(2 * DEPTH, doc_hi), onehot(128, doc_lo),
                            (((1,), (1,)), ((), ())), preferred_element_type=jnp.float32)
    marks = jnp.concatenate([marks[:DEPTH], marks[DEPTH:]], axis=1)
    ranks = prefix_rank(marks)
    doc_rank = jnp.zeros((8, 128), jnp.float32)
    for h in range(2):
        for d in range(DEPTH):
            line = jnp.broadcast_to(ranks[d:d + 1, h * 128:(h + 1) * 128], (8, 128))
            doc_rank = jnp.where(
                doc_hi == h * DEPTH + d, jnp.take_along_axis(line, doc_lo, axis=1), doc_rank)
    doc_rank = doc_rank.astype(jnp.int32)
    row_id = lax.broadcasted_iota(jnp.int32, (PACK, CHIP_SLOTS), 0)
    for d in range(1, DEPTH):
        ms[d] = marks[d:d + 1]

    def mark_copy(d):
        return pltpu.make_async_remote_copy(
            src_ref=ms.at[d], dst_ref=mr.at[d], send_sem=mss, recv_sem=mrs,
            device_id={"shard": z_dev[d]})

    def z_copy(d):
        return pltpu.make_async_remote_copy(
            src_ref=zs.at[d], dst_ref=zr.at[d], send_sem=zss.at[d], recv_sem=zrs.at[d],
            device_id={"shard": z_dev[d]})

    def spread(d, part, rows, column):
        low = part[-1] * 16
        rows = mark_absent(rows, column[low:low + 64])
        ps[d, part[-1]:part[-1] + 4] = rows.reshape(4, 2, CL, HALF).astype(jnp.bfloat16)
        for p in part:
            if p == 0:
                pltpu.make_async_remote_copy(
                    src_ref=ps.at[d, 0, 1 - rep], dst_ref=pr.at[d, 0, rep], send_sem=psc.at[d],
                    recv_sem=prc.at[d], device_id={"rep": 1 - rep}).start()
                pr[d, 0, rep] = ps[d, 0, rep]
                continue
            for r in range(2):
                pltpu.make_async_remote_copy(
                    src_ref=ps.at[d, p, r], dst_ref=pr.at[d, p, rep], send_sem=pss.at[d],
                    recv_sem=prs.at[d], device_id={"shard": p_dev[p], "rep": r}).start()

    def pack(group):
        select = jnp.concatenate(
            [onehot(PACK, jnp.where(doc_z == d, doc_rank, -1)) for d in group], axis=0)
        rows = jnp.dot(select, e_ref[...], preferred_element_type=jnp.float32)
        for i, d in enumerate(group):
            zs[d] = rows[i * PACK:(i + 1) * PACK].astype(jnp.bfloat16)

    load.wait()
    for group in PAIRS:
        pack(group)
    pl.semaphore_wait(barrier, 2 * (DEPTH - 1) + 2 * (PLANE - 1) + 1)
    for d in FAR_Z:
        mark_copy(d).start()
    for d in ORDER:
        z_copy(d).start()
    rows = jnp.dot(onehot(CHIP_SLOTS, jnp.where(doc_z == 0, doc_chip, -1)), e_ref[...],
                   preferred_element_type=jnp.float32)
    column = mark_column(jnp.where(marks[:1] > 0.0, 0, -1))
    for part in FAR_PARTS:
        spread(0, part, rows[part[-1] * 16:part[-1] * 16 + 64], column)

    others = pl.ds(1, PLANE - 1)
    around = pl.ds(1, DEPTH - 1)
    pltpu.make_async_copy(mr.at[around], mr.at[around], mrs).wait()
    there = jnp.concatenate([jnp.zeros((1, CHIP_SLOTS), jnp.float32)]
                            + [mr[d] for d in range(1, DEPTH)], axis=0)
    ranks = prefix_rank(there)
    full = jnp.max(ranks + there)
    ranks = jnp.where(there > 0.0, ranks, -1.0).astype(jnp.int32)

    place = lax.broadcasted_iota(jnp.int32, (CHIP_SLOTS, PACK), 1)

    def expand(d):
        column = mark_column(ranks[d:d + 1])
        wide = jnp.concatenate([column, column[:, :PACK - 128]], axis=1)
        select = jnp.where(place == wide, 1.0, 0.0).astype(jnp.bfloat16)
        pltpu.make_async_copy(zr.at[d], zr.at[d], zrs.at[d]).wait()
        rows = jnp.dot(select, zr[d], preferred_element_type=jnp.float32)
        for part in FAR_PARTS:
            spread(d, part, rows[part[-1] * 16:part[-1] * 16 + 64], column)

    i = lax.broadcasted_iota(jnp.int32, (SLOTS, SLOTS), 0)
    j = lax.broadcasted_iota(jnp.int32, (SLOTS, SLOTS), 1)
    same = i % CL == j % CL
    same_off = same & (i != j)

    def masked(a, b, mask):
        gram = lax.dot_general(a, b, (((1,), (1,)), ((), ())),
                               preferred_element_type=jnp.float32)
        ok = mask & (gram == gram)
        return jnp.where(ok, jnp.exp(sharpness * (gram - 1.0)), 0.0)

    totals = {}
    done = []

    def process(d):
        k = len(done)
        pltpu.make_async_copy(pr.at[d, others], pr.at[d, others], prs.at[d]).wait()
        pltpu.make_async_copy(pr.at[d, 0, 1 - rep], pr.at[d, 0, 1 - rep], prc.at[d]).wait()
        sides = [pr[d, :, f].astype(jnp.float32).reshape(SLOTS, HALF) for f in range(2)]
        square = jnp.sum(sides[0] * sides[0] + sides[1] * sides[1], axis=1, keepdims=True)
        scale = lax.rsqrt(square + epsilon)
        new = jnp.concatenate([(v * scale).astype(jnp.bfloat16) for v in sides], axis=1)
        unit[k * SLOTS:(k + 1) * SLOTS] = new
        both = jnp.concatenate([same] * k + [same_off], axis=0)
        grid = masked(unit[:(k + 1) * SLOTS], new, both)
        totals[d] = jnp.sum(grid, axis=0, keepdims=True)
        for n, e in enumerate(done):
            back = grid[n * SLOTS:(n + 1) * SLOTS].T
            totals[e] += jnp.sum(back, axis=0, keepdims=True)
        done.append(d)

    expand(1)
    expand(7)
    process(0)
    expand(2)
    expand(6)
    process(1)
    process(7)
    expand(3)
    expand(5)
    process(2)
    process(6)
    expand(4)
    process(3)
    process(5)
    process(4)

    table = jnp.concatenate([totals[d] for d in range(DEPTH)], axis=0)
    table = jnp.where(full > float(PACK), -1.0, table)
    for d in range(DEPTH):
        tot[d] = table[d:d + 1]

    for d in FAR_Z:
        for r in range(2):
            pltpu.make_async_remote_copy(
                src_ref=tot.at[d], dst_ref=r1.at[d, rep], send_sem=r1s, recv_sem=r1r,
                device_id={"shard": z_dev[(DEPTH - d) % DEPTH], "rep": r}).start()
    across = pltpu.make_async_remote_copy(
        src_ref=tot.at[0], dst_ref=r1.at[0, rep], send_sem=r1c.at[0], recv_sem=r1c.at[1],
        device_id={"rep": 1 - rep})
    across.start()
    r1[0, rep] = table[:1]
    pltpu.make_async_copy(r1.at[around], r1.at[around], r1r).wait()
    across.wait()

    lane = lax.broadcasted_iota(jnp.int32, (8, SLOTS), 1)
    base = lax.broadcasted_iota(jnp.int32, (8, SLOTS), 0) * CL + lane % CL
    for h, far in ((1, (10, 9, 11, 8, 14, 13, 15, 12)), (0, (6, 2, 5, 7, 4, 1, 3, 0))):
        block = jnp.zeros((8, SLOTS), jnp.float32)
        for n in range(2 * DEPTH):
            line = jnp.broadcast_to(r1[n // 2, n % 2], (8, SLOTS))
            moved = jnp.take_along_axis(line, base + h * 64, axis=1)
            block = jnp.where(lane // CL == n, moved, block)
        for p in far:
            s2[p] = block[p % 8:p % 8 + 1]
        for p in far:
            if p == 0:
                r2[0] = block[:1]
                continue
            pltpu.make_async_remote_copy(
                src_ref=s2.at[p], dst_ref=r2.at[p], send_sem=r2s, recv_sem=r2r,
                device_id={"shard": p_dev[(4 - p // 4) % 4 * 4 + (4 - p % 4) % 4]}).start()
    for d in ORDER:
        pltpu.make_async_copy(zs.at[d], zs.at[d], zss.at[d]).wait()
    for d in range(DEPTH):
        pltpu.make_async_copy(ps.at[d, others], ps.at[d, others], pss.at[d]).wait()
        pltpu.make_async_copy(ps.at[d, 0, 1 - rep], ps.at[d, 0, 1 - rep], psc.at[d]).wait()
    pltpu.make_async_copy(ms.at[around], ms.at[around], mss).wait()
    pltpu.make_async_copy(r1.at[around], r1.at[around], r1s).wait()
    pltpu.make_async_copy(r2.at[others], r2.at[others], r2r).wait()

    value = jnp.zeros((8, 128), jnp.float32)
    least = jnp.zeros((1, SLOTS), jnp.float32)
    doc_lane = doc_z * 16 + labels % 16
    for p in range(PLANE):
        line = r2[p]
        least = jnp.minimum(least, line)
        found = jnp.take_along_axis(jnp.broadcast_to(line, (8, 128)), doc_lane, axis=1)
        value = jnp.where(doc_p == p, found, value)
    out_ref[...] = value
    flag_ref[0] = jnp.where(jnp.min(least) < 0.0, 1, 0).astype(jnp.int32)

    pltpu.make_async_copy(s2.at[others], s2.at[others], r2s).wait()


def packed_totals(embeddings, labels):
    dma = pltpu.SemaphoreType.DMA
    return pl.pallas_call(
        packed_kernel,
        out_shape=(jax.ShapeDtypeStruct((8, 128), jnp.float32),
                   jax.ShapeDtypeStruct((1,), jnp.int32)),
        in_specs=[pl.BlockSpec(memory_space=pl.ANY)] * 2,
        out_specs=(pl.BlockSpec(memory_space=pltpu.VMEM), pl.BlockSpec(memory_space=pltpu.SMEM)),
        scratch_shapes=[
            pltpu.VMEM((DOCS_DEV, HALF), jnp.bfloat16),
            pltpu.VMEM((8, 128), jnp.int32),
            pltpu.VMEM((DEPTH, PACK, HALF), jnp.bfloat16),
            pltpu.VMEM((DEPTH, PACK, HALF), jnp.bfloat16),
            pltpu.VMEM((DEPTH, 1, CHIP_SLOTS), jnp.float32),
            pltpu.VMEM((DEPTH, 1, CHIP_SLOTS), jnp.float32),
            pltpu.VMEM((DEPTH, PLANE, 2, CL, HALF), jnp.bfloat16),
            pltpu.VMEM((DEPTH, PLANE, 2, CL, HALF), jnp.bfloat16),
            pltpu.VMEM((DEPTH * SLOTS, D), jnp.bfloat16),
            pltpu.VMEM((DEPTH, 1, SLOTS), jnp.float32),
            pltpu.VMEM((DEPTH, 2, 1, SLOTS), jnp.float32),
            pltpu.VMEM((PLANE, 1, SLOTS), jnp.float32),
            pltpu.VMEM((PLANE, 1, SLOTS), jnp.float32),
            dma((2,)), dma, dma, dma((DEPTH,)), dma((DEPTH,)), dma((DEPTH,)), dma((DEPTH,)),
            dma((DEPTH,)), dma((DEPTH,)), dma, dma, dma((2,)), dma, dma,
        ],
        compiler_params=pltpu.CompilerParams(
            collective_id=1, has_side_effects=True, vmem_limit_bytes=60 * 1024 * 1024),
        name="packed_totals",
    )(embeddings, labels.reshape(8, 128))


def local(embeddings, labels):
    totals, overflow = packed_totals(embeddings, labels)
    totals = lax.cond(
        overflow[0] > 0, lambda: direct_totals(embeddings, labels), lambda: totals)
    return jnp.log1p(totals.reshape(DOCS_DEV))


def solution(mesh):
    return jax.shard_map(
        local,
        mesh=mesh,
        in_specs=(P("shard", None), P("shard")),
        out_specs=P("shard"),
        check_vma=False,
    )
```
